128 devices in a mesh: gx: 16 (over z, y), gy: 8 (over x, core).
Axes of the slice: x: 4, y: 4, z: 4, core: 2. Of those that a mesh axis runs over, the one named last changes fastest.
Arguments:
- coarse: float32 [5, 2, 2048, 2048], P(None, None, 'gx', 'gy'), may hold values from -6 to 6
- fine_old: float32 [7936, 5, 4, 1024], P(('gx', 'gy')), may hold values from -6 to 6
- old_count: int32 [128], P(('gx', 'gy')), may hold values from 0 to 62, as said below
- box_coords: int32 [2, 7936], P(None, ('gx', 'gy')), may hold values from 1 to 126, as said below
- new_owner: int32 [7936], P(('gx', 'gy')), may hold values from 0 to 127, as said below
- new_slot: int32 [7936], P(('gx', 'gy')), may hold values from 0 to 31, as said below
- fresh_box: int32 [7936], P(('gx', 'gy')), may hold values 0 or 1
Outputs:
- coarse_new: float32 [5, 2, 2048, 2048], P(None, None, 'gx', 'gy')
- fine_new: float32 [4096, 5, 4, 1024], P(('gx', 'gy'))
The draws below stay inside these ranges and needn't reach their ends.
Inputs may be any that keep to these rules, and one draw needn't show every extreme that they name: `old_count`: the slots of a device below its count hold its boxes; in every column of devices with one gy index one device holds exactly 62. `box_coords`: A live box's footprint lies in the region of the device that holds it in the old layout, off the outermost cycle of footprints of that region; footprints of one device's live boxes are distinct. Entries of slots that are not live are arbitrary within the range. `new_owner`: A live box's new device has the same gy index as its old device; one device hands at most 2 boxes to any one other device, and exactly that many in some pairs; every device receives exactly 32 live boxes, its own that stay included. Entries of slots that are not live are arbitrary within the range. `new_slot`: the live boxes that go to one device take each of its 32 slots exactly once.
All inputs are finite; a program needn't handle non-finite values. No bound on the sum of `fresh_box` on one device may be relied on, other than what follows from the above.
Results may differ from the reference program's by a relative error of at most 0.0003.
Values sent between devices are 32-bit elements; how exact they have to be, the bound alone decides.
No kernel may reach another device: no remote copies, remote signals or barrier semaphores. Data moves between devices by JAX's collectives and lax.ppermute only.
A program may use at most 640 MiB of HBM per device.

```python
import jax
import jax.numpy as jnp
from jax import lax

FIELDS = 5
BX = 32
BZ = 4
CX = 128
CY = 256
BOX_DEV = 32
MOVE_CAP = 2
CZ = 2
OLD_CAP = 62
NX = 2048
NY = 2048
SLOT_TOTAL = 7936
N_GX = 16
N_GY = 8
DEVICES = 128


def layout(key):
    row_count = N_GY
    col_count = N_GX
    slot_count = OLD_CAP
    keys = jax.random.split(key, 6)
    heavy = jax.random.randint(keys[0], (row_count,), 0, col_count)
    rolls = jax.random.randint(keys[1], (row_count, col_count, col_count), 0, 10)
    flow = (rolls >= 2).astype(jnp.int32) + (rolls >= 6).astype(jnp.int32)
    column_ids = jnp.arange(col_count)
    from_heavy = column_ids[None, :, None] == heavy[:, None, None]
    to_heavy = column_ids[None, None, :] == heavy[:, None, None]
    diagonal = (column_ids[:, None] == column_ids[None, :])[None]
    flow = jnp.where(from_heavy, MOVE_CAP, flow)
    flow = jnp.where(to_heavy | diagonal, 0, flow)
    inflow = jnp.sum(flow, axis=1)
    stay_count = BOX_DEV - inflow
    demand = flow + diagonal.astype(jnp.int32) * stay_count[:, :, None]
    counts = jnp.sum(demand, axis=2)
    slot_ids = jnp.arange(slot_count)
    ends = jnp.cumsum(demand, axis=2)
    sorted_dest = jnp.sum((slot_ids[None, None, :, None] >= ends[:, :, None, :]).astype(jnp.int32), axis=3)
    is_live = slot_ids[None, None, :] < counts[:, :, None]
    score = jax.random.randint(keys[2], (row_count, col_count, slot_count), 0, 1 << 20) * slot_count + slot_ids
    score = jnp.where(is_live, score, (1 << 30) + slot_ids)
    order = jnp.argsort(score, axis=2, stable=True)
    dest_column = jnp.take_along_axis(sorted_dest, order, axis=2)
    same_dest = (dest_column[:, :, :, None] == dest_column[:, :, None, :]) & (slot_ids[:, None] > slot_ids[None, :])
    move_rank = jnp.sum(same_dest.astype(jnp.int32), axis=3)
    before = jnp.cumsum(demand, axis=1) - demand
    offset_at = jnp.take_along_axis(before, jnp.minimum(dest_column, col_count - 1), axis=2)
    slot_new = offset_at + move_rank
    spare_slot = jax.random.randint(keys[3], (row_count, col_count, slot_count), 0, BOX_DEV)
    spare_dest = jax.random.randint(keys[4], (row_count, col_count, slot_count), 0, col_count)
    slot_new = jnp.where(is_live, slot_new, spare_slot)
    dest_column = jnp.where(is_live, dest_column, spare_dest)
    owner = dest_column * row_count + jnp.arange(row_count)[:, None, None]
    owner = jnp.transpose(owner, (1, 0, 2)).reshape(-1).astype(jnp.int32)
    slot_new = jnp.transpose(slot_new, (1, 0, 2)).reshape(-1).astype(jnp.int32)
    counts = jnp.transpose(counts).reshape(-1).astype(jnp.int32)
    across = CX // (BX // 2)
    along = CY // (BX // 2)
    inner_count = (across - 2) * (along - 2)
    pick = jax.random.randint(keys[5], (col_count, row_count, inner_count), 0, 1 << 20) * inner_count + jnp.arange(inner_count)
    chosen = jnp.argsort(pick, axis=2, stable=True)[:, :, :slot_count]
    foot_x = 1 + chosen // (along - 2) + jnp.arange(col_count)[:, None, None] * across
    foot_y = 1 + chosen % (along - 2) + jnp.arange(row_count)[None, :, None] * along
    coords = jnp.stack([foot_x.reshape(-1), foot_y.reshape(-1)]).astype(jnp.int32)
    return (counts, coords, owner, slot_new)


def draw_old_count(key, part):
    shared = layout(key)
    return shared[0]


def draw_box_coords(key, part):
    shared = layout(key)
    return shared[1]


def draw_new_owner(key, part):
    shared = layout(key)
    return shared[2]


def draw_new_slot(key, part):
    shared = layout(key)
    return shared[3]


def touch_ends(drawn, key, smallest, high):
    extent = drawn.shape
    place = [jax.random.randint(jax.random.fold_in(key, axis), (), 0, extent[axis]) for axis in range(len(extent))]
    drawn = drawn.at[tuple(place)].set(smallest)
    longest = extent.index(max(extent))
    place[longest] = (place[longest] + 1) % extent[longest]
    return drawn.at[tuple(place)].set(high)


def block_scale(key, dims, cuts, smallest, largest):
    def one(axis_at, parts):
        steps = jax.random.uniform(jax.random.fold_in(jax.random.fold_in(key, 6), axis_at), (parts,), jnp.float32, smallest / len(cuts), largest / len(cuts))
        return jnp.repeat(jnp.exp(steps), dims[axis_at] // parts).reshape((-1,) + (1,) * (len(dims) - axis_at - 1))

    loudness = one(*cuts[0])
    for cut in cuts[1:]:
        loudness = loudness * one(*cut)
    return loudness


def scatter_about(stream_key, extent, width, most, pieces=(), held_as=jnp.bfloat16):
    loudness = block_scale(stream_key, extent, pieces, -0.22, 0.18) if pieces else 1.0
    values = jax.random.normal(stream_key, extent, jnp.float32) * width * loudness
    return jnp.minimum(jnp.maximum(values, -most), most).astype(held_as)


def setup_inputs(seed: int = 0) -> dict:
    key_of = jax.random.split(jax.random.key(seed), 8)
    return {
        "coarse": scatter_about(key_of[0], (FIELDS, CZ, NX, NY), 1.0, 6.0, ((2, 16), (3, 8)), jnp.float32),
        "fine_old": scatter_about(key_of[1], (SLOT_TOTAL, FIELDS, BZ, BX * BX), 1.0, 6.0, ((0, 128),), jnp.float32),
        "old_count": draw_old_count(jax.random.fold_in(key_of[7], 71), 0),
        "box_coords": draw_box_coords(jax.random.fold_in(key_of[7], 71), 0),
        "new_owner": draw_new_owner(jax.random.fold_in(key_of[7], 71), 0),
        "new_slot": draw_new_slot(jax.random.fold_in(key_of[7], 71), 0),
        "fresh_box": touch_ends((jax.random.randint(key_of[6], (SLOT_TOTAL,), 0, 4) < 1).astype(jnp.int32), jax.random.fold_in(key_of[6], 1), 0, 1),
    }


COURANT = ((0.10, 0.20, -0.12), (-0.08, -0.15, 0.20), (0.12, 0.10, 0.18), (-0.05, 0.22, -0.15), (0.15, -0.18, -0.10))


def speeds(scale):
    table = jnp.array(COURANT, jnp.float32) * scale
    return jnp.maximum(table, 0.0)[:, :, None, None, None], jnp.minimum(table, 0.0)[:, :, None, None, None]


def face_fluxes(padded, scale):
    ahead, behind = speeds(scale)
    inner_cells = padded[..., 1:-1, 1:-1]
    flux_z = ahead[:, 0] * jnp.roll(inner_cells, 1, axis=-3) + behind[:, 0] * inner_cells
    flux_x = ahead[:, 1] * padded[..., :-1, 1:-1] + behind[:, 1] * padded[..., 1:, 1:-1]
    flux_y = ahead[:, 2] * padded[..., 1:-1, :-1] + behind[:, 2] * padded[..., 1:-1, 1:]
    return flux_z, flux_x, flux_y


def change(fluxes):
    flux_z, flux_x, flux_y = fluxes
    return -(jnp.roll(flux_z, -1, axis=-3) - flux_z) - (flux_x[..., 1:, :] - flux_x[..., :-1, :]) - (flux_y[..., 1:] - flux_y[..., :-1])


def spread(values):
    return values[..., :, None, :, None, :, None]


def interpolate(box_patch):
    centre = box_patch[..., 1:-1, 1:-1]
    slope_x = 0.5 * (box_patch[..., 2:, 1:-1] - box_patch[..., :-2, 1:-1])
    slope_y = 0.5 * (box_patch[..., 1:-1, 2:] - box_patch[..., 1:-1, :-2])
    slope_z = 0.5 * (jnp.roll(centre, -1, axis=-3) - jnp.roll(centre, 1, axis=-3))
    sign_pair = jnp.array([-1.0, 1.0], jnp.float32)
    children = spread(centre) + 0.25 * (spread(slope_z) * sign_pair[:, None, None, None, None] + spread(slope_x) * sign_pair[:, None, None] + spread(slope_y) * sign_pair)
    dims_in = centre.shape
    children = children.reshape(dims_in[:-3] + (2 * dims_in[-3], 2 * dims_in[-2], 2 * dims_in[-1]))
    return children[..., 1:-1, 1:-1]


def coarsen_face(values):
    dims_in = values.shape
    return 0.25 * jnp.sum(values.reshape(dims_in[:-2] + (dims_in[-2] // 2, 2, dims_in[-1] // 2, 2)), axis=(-3, -1))


def advance(box_start, box_patch, fresh_flag):
    ghost_cycle = interpolate(box_patch)
    inside = ghost_cycle[..., 1:-1, 1:-1]
    is_fresh = (fresh_flag > 0)[..., None, None, None, None]
    box_state = jnp.where(is_fresh, inside, box_start)
    first_flux = face_fluxes(ghost_cycle.at[..., 1:-1, 1:-1].set(box_state), 2.0)
    middle = box_state + change(first_flux)
    second = face_fluxes(ghost_cycle.at[..., 1:-1, 1:-1].set(middle), 2.0)
    final_state = 0.5 * (box_state + (middle + change(second)))
    mean_x = 0.5 * (first_flux[1] + second[1])
    mean_y = 0.5 * (first_flux[2] + second[2])
    face_means = jnp.stack([coarsen_face(mean_x[..., 0, :]), coarsen_face(mean_x[..., -1, :]), coarsen_face(mean_y[..., 0]), coarsen_face(mean_y[..., -1])], axis=-4)
    dims_in = final_state.shape
    blocks = final_state.reshape(dims_in[:-3] + (dims_in[-3] // 2, 2, dims_in[-2] // 2, 2, dims_in[-1] // 2, 2))
    box_average = 0.125 * jnp.sum(blocks, axis=(-5, -3, -1))
    return final_state, box_average, face_means


def settle(updated, low_x, low_y, has_box, avg_grid, sum_x, count_x, sum_y, count_y):
    fields, depth_cells, width_x, width_y = updated.shape
    across_count, along_count = has_box.shape
    half_box = width_x // across_count
    coarse_x = low_x.reshape(fields, depth_cells, across_count, half_box, along_count, half_box)[:, :, :, 0]
    rows_x = jnp.transpose(sum_x, (2, 3, 0, 1, 4)) - count_x[:, :, None] * coarse_x
    zeros_x = jnp.zeros((fields, depth_cells, across_count, half_box - 1, along_count, half_box), updated.dtype)
    jump_x = jnp.concatenate([rows_x[:, :, :, None], zeros_x], axis=3).reshape(updated.shape)
    coarse_y = low_y.reshape(fields, depth_cells, across_count, half_box, along_count, half_box)[..., 0]
    rows_y = jnp.transpose(sum_y, (2, 3, 0, 4, 1)) - count_y[:, None, :] * coarse_y
    zeros_y = jnp.zeros((fields, depth_cells, across_count, half_box, along_count, half_box - 1), updated.dtype)
    jump_y = jnp.concatenate([rows_y[..., None], zeros_y], axis=5).reshape(updated.shape)
    corrected = updated - (jnp.roll(jump_x, -1, axis=2) - jump_x) - (jnp.roll(jump_y, -1, axis=3) - jump_y)
    spread_avg = jnp.transpose(avg_grid, (2, 3, 0, 4, 1, 5)).reshape(updated.shape)
    covered = jnp.repeat(jnp.repeat(has_box > 0.5, half_box, axis=0), half_box, axis=1)
    return jnp.where(covered, spread_avg, corrected)


def wrap_rim(values):
    return jnp.pad(values, ((0, 0), (0, 0), (1, 1), (1, 1)), mode="wrap")


def reference(coarse, fine_old, old_count, box_coords, new_owner, new_slot, fresh_box):
    half_box = BX // 2
    fields, depth_cells, width_x, width_y = coarse.shape
    slot_total = fine_old.shape[0]
    box_total = BOX_DEV * DEVICES
    slot_ids = jnp.arange(slot_total, dtype=jnp.int32)
    holder = slot_ids // OLD_CAP
    is_live = (slot_ids % OLD_CAP) < old_count[holder]
    target = jnp.where(is_live, new_owner * BOX_DEV + new_slot, box_total)
    source = jnp.zeros((box_total,), jnp.int32).at[target].set(slot_ids, mode="drop")

    def one_box(box_index):
        corner_x = box_coords[0, box_index] * half_box - 2
        corner_y = box_coords[1, box_index] * half_box - 2
        box_patch = lax.dynamic_slice(coarse, (jnp.int32(0), jnp.int32(0), corner_x, corner_y), (fields, depth_cells, half_box + 4, half_box + 4))
        box_start = fine_old[box_index].reshape(fields, BZ, BX, BX)
        return advance(box_start, box_patch, fresh_box[box_index])

    final_state, box_average, face_means = lax.map(one_box, source)
    fine_new = final_state.reshape(box_total, fields, BZ, BX * BX)

    first_flux = face_fluxes(wrap_rim(coarse), 1.0)
    middle = coarse + change(first_flux)
    second = face_fluxes(wrap_rim(middle), 1.0)
    updated = 0.5 * (coarse + (middle + change(second)))
    low_x = (0.5 * (first_flux[1] + second[1]))[:, :, :-1]
    low_y = (0.5 * (first_flux[2] + second[2]))[..., :-1]

    across = box_coords[0, source]
    along = box_coords[1, source]
    across_count = width_x // half_box
    along_count = width_y // half_box
    zero_grid = jnp.zeros((across_count, along_count), jnp.float32)
    has_box = zero_grid.at[across, along].add(1.0)
    count_x = zero_grid.at[across, along].add(1.0).at[across + 1, along].add(1.0)
    count_y = zero_grid.at[across, along].add(1.0).at[across, along + 1].add(1.0)
    avg_grid = jnp.zeros((across_count, along_count, fields, depth_cells, half_box, half_box), jnp.float32).at[across, along].add(box_average)
    face_zero = jnp.zeros((across_count, along_count, fields, depth_cells, half_box), jnp.float32)
    sum_x = face_zero.at[across, along].add(face_means[:, 0]).at[across + 1, along].add(face_means[:, 1])
    sum_y = face_zero.at[across, along].add(face_means[:, 2]).at[across, along + 1].add(face_means[:, 3])
    coarse_new = settle(updated, low_x, low_y, has_box, avg_grid, sum_x, count_x, sum_y, count_y)
    return coarse_new, fine_new
```

```python
import jax
import jax.numpy as jnp
import numpy as np
import ml_dtypes
from jax import lax
from jax.experimental import pallas as pl
from jax.experimental.pallas import tpu as pltpu
from jax.sharding import PartitionSpec as P

BX = 32
BZ = 4
HALF = 16
BOX_DEV = 32
MOVE_CAP = 2
FIELDS = 5
CHUNK = 8

COURANT = (
    (0.1, 0.2, -0.12),
    (-0.08, -0.15, 0.2),
    (0.12, 0.1, 0.18),
    (-0.05, 0.22, -0.15),
    (0.15, -0.18, -0.1),
)
CX, CY, OLD_CAP = 128, 256, 62
ROWS = FIELDS * BX


def sign(value):
    return 1 if value > 0 else -1


def first_row(sx):
    return -2 if sx > 0 else -1


def patch_maps(sx, sy):
    maps = np.zeros((128, 6, 128), np.float32)
    start = first_row(sx)

    def put(block, lane, row, col, value):
        maps[(row - start) * 20 + col, block, lane] += value

    def child(block, lane, row, col, b, e):
        put(block, lane, row, col, 1.0)
        if b:
            put(block, lane, row + 1, col, b / 8)
            put(block, lane, row - 1, col, -b / 8)
        if e:
            put(block, lane, row, col + 1, e / 8)
            put(block, lane, row, col - 1, -e / 8)

    for lane in range(128):
        xg, y = divmod(lane, 32)
        b = 1 if xg % 2 else -1
        e = 1 if y % 2 else -1
        child(0, lane, xg // 2, 2 + y // 2, b, e)
        if sx > 0 and xg == 0:
            child(1, lane, -1, 2 + y // 2, 1, e)
        if sx < 0 and xg == 3:
            child(1, lane, 2, 2 + y // 2, -1, e)
        if sy > 0 and y == 0:
            child(2, lane, xg // 2, 1, b, 1)
        if sy < 0 and y == 31:
            child(2, lane, xg // 2, 18, b, -1)
        child(3, lane, -1 if sx > 0 else 2, 2 + lane % 16, sx, 0)
        for xc in range(2):
            child(4 + xc, lane, xc, 1 if sy > 0 else 18, 0, sy)
    flat = maps.reshape(128, 768)
    return np.concatenate([flat, flat])


def mean_map():
    maps = np.zeros((128, 2, 128), np.float32)
    for source in range(128):
        xg, y = divmod(source, 32)
        for lane in range(128):
            if lane % 16 == y // 2:
                maps[source, xg // 2, lane] = 0.125
    flat = maps.reshape(128, 256)
    return np.concatenate([flat, flat])


def face_map(sx, sy):
    maps = np.zeros((128, 3, 128), np.float32)
    for source in range(128):
        xg, y = divmod(source, 32)
        for lane in range(128):
            if xg == (3 if sx > 0 else 0) and lane % 16 == y // 2:
                maps[source, 0, lane] = 0.25
            if y == (31 if sy > 0 else 0):
                maps[source, 1 + xg // 2, lane] = 0.25
    flat = maps.reshape(128, 384)
    return np.concatenate([flat, flat])


def all_maps():
    grow = np.stack([patch_maps(sign(c[1]), sign(c[2])) for c in COURANT])
    face = np.stack([face_map(sign(c[1]), sign(c[2])) for c in COURANT])
    half = ml_dtypes.bfloat16
    return grow.astype(half), mean_map().astype(half), face.astype(half)


GROW, MEAN, FACE = all_maps()


def lanes():
    return lax.broadcasted_iota(jnp.int32, (8, 128), 1)


def sublanes():
    return lax.broadcasted_iota(jnp.int32, (8, 128), 0)


def base_copies(coarse, windows, sem):
    return [
        pltpu.make_async_copy(coarse.at[:, :, :, pl.ds(64 * w, 128)], windows.at[w], sem.at[w])
        for w in (0, 2)
    ]


def cut_middle(windows):
    def rows(step, carry):
        at = pl.ds(pl.multiple_of(step * 16, 16), 16)
        lane = lax.broadcasted_iota(jnp.int32, (16, 128), 1)
        for f in range(FIELDS):
            for z in range(2):
                both = jnp.where(lane < 64, windows[2, f, z, at, :], windows[0, f, z, at, :])
                windows[1, f, z, at, :] = pltpu.roll(both, 64, 1)
        return carry

    lax.fori_loop(0, CX // 16, rows, 0)


def split_store(target, f, at, value):
    high = value.astype(jnp.bfloat16)
    target[f, at, 0:128] = high
    target[f, at, 128:256] = (value - high.astype(jnp.float32)).astype(jnp.bfloat16)


def pack(windows, packed, j, bx, by):
    which = (by >= 7).astype(jnp.int32) + (by >= 9).astype(jnp.int32)
    start = by * HALF - 2 - which * 64
    lane = lanes()
    shifts = [lax.rem(20 * i - start + 256, 128) for i in range(5)]
    for f in range(FIELDS):
        first = first_row(sign(COURANT[f][1]))
        both = []
        for z in range(2):
            held = None
            for i in range(5):
                row = windows[which, f, z, pl.ds(bx * HALF + first + i, 8, stride=2), :]
                row = pltpu.roll(row, shifts[i], 1)
                held = row if held is None else jnp.where(lane < 20 * i, held, row)
            both.append(held)
        at = pl.ds(pl.multiple_of(j * 16, 16), 16)
        split_store(packed, f, at, jnp.concatenate(both, axis=0))


def z_children(values):
    count = len(values)
    out = []
    for z in range(count):
        tilt = 0.125 * (values[(z + 1) % count] - values[(z - 1) % count])
        out += [values[z] - tilt, values[z] + tilt]
    return out


def fill_fresh(boxes, slot, grown, j):
    for f in range(FIELDS):
        parts = [grown[f, pl.ds(pl.multiple_of(j * 16 + 8 * z, 8), 8), 0:128] for z in range(2)]
        for z, value in enumerate(z_children(parts)):
            boxes[slot, pl.ds(32 * f + z, 8, stride=4), :] = value


def upwind(values, sx, sy, sz, lane):
    out = []
    for z in range(BZ):
        v = values[z]
        vz = values[(z - sz) % BZ]
        if sx > 0:
            near = pltpu.roll(v, 32, 1)
            xs = jnp.where(lane < 32, pltpu.roll(near, 1, 0), near)
        else:
            near = pltpu.roll(v, 96, 1)
            xs = jnp.where(lane >= 96, pltpu.roll(near, 7, 0), near)
        ys = pltpu.roll(v, 1 if sy > 0 else 127, 1)
        out.append((vz, xs, ys))
    return out


def advance_field(boxes, slot, grown, j, f):
    cz, cx, cy = COURANT[f]
    sz, sx, sy = sign(cz), sign(cx), sign(cy)
    az, ax, ay = 2 * abs(cz), 2 * abs(cx), 2 * abs(cy)
    total = az + ax + ay
    lane, sub = lanes(), sublanes()
    edge_x = ((sub == 0) & (lane < 32)) if sx > 0 else ((sub == 7) & (lane >= 96))
    edge_y = (lane % 32) == (0 if sy > 0 else 31)
    ghost_x = jnp.where(edge_x, ax, 0.0)
    gain_x = jnp.where(edge_x, 0.0, ax)
    gain_y = jnp.where(edge_y, 0.0, ay)
    rims = []
    for z in range(2):
        at = pl.ds(pl.multiple_of(j * 16 + 8 * z, 8), 8)
        rims.append(ghost_x * grown[f, at, 128:256] + ay * grown[f, at, 256:384])
    rims = z_children(rims)
    state = [boxes[slot, pl.ds(32 * f + z, 8, stride=4), :] for z in range(BZ)]
    middle = []
    half_x, half_y = 0.5 * gain_x, 0.5 * gain_y
    for z, (vz, xs, ys) in enumerate(upwind(state, sx, sy, sz, lane)):
        middle.append(
            (1 - 0.5 * total) * state[z]
            + (0.5 * az) * vz
            + half_x * xs
            + half_y * ys
            + 0.5 * rims[z]
        )
    final = []
    for z, (vz, xs, ys) in enumerate(upwind(middle, sx, sy, sz, lane)):
        final.append(
            (state[z] + rims[z]) - total * middle[z] + az * vz + gain_x * xs + gain_y * ys
        )
    for z in range(BZ):
        boxes[slot, pl.ds(32 * f + z, 8, stride=4), :] = final[z]
    return middle, final


def grow(packed, maps, grown, width):
    for f in range(FIELDS):
        grown[f, :, 0:width] = jnp.dot(
            packed[f], maps[f][:, 0:width], preferred_element_type=jnp.float32
        )


def fetch_all(pairs, sem):
    copies = [
        pltpu.make_async_copy(source, target, sem.at[i]) for i, (source, target) in enumerate(pairs)
    ]
    for copy in copies:
        copy.start()
    for copy in copies:
        copy.wait()


def send_kernel(
    count_in, coords_in, owner_in, slots_in, fresh_in, coarse, maps_in, fine, send,
    count, coords, owner, slots, fresh, maps,
    windows, packed, grown, boxes, info, order, target, rank, ranks,
    int_sem, base_sem, map_sem, info_sem, get_sem, put_sem,
):
    here_x, here_y = lax.axis_index("gx"), lax.axis_index("gy")
    column = lax.axis_size("gy")
    base = base_copies(coarse, windows, base_sem)
    for copy in base:
        copy.start()
    bring_maps = pltpu.make_async_copy(maps_in, maps, map_sem)
    bring_maps.start()
    fetch_all(
        [
            (count_in, count), (owner_in, owner), (slots_in, slots), (coords_in, coords),
            (fresh_in, fresh),
        ],
        int_sem,
    )
    for i in range(16):
        ranks[i] = 0
        info[i] = jnp.full((8, 128), -1.0, jnp.float32)

    def sort(i, n):
        dest = lax.div(owner[i], column)
        goes = dest != here_x

        @pl.when(goes)
        def _():
            pltpu.make_async_copy(fine.at[i], boxes.at[n], get_sem.at[n]).start()
            r = ranks[dest]
            order[n] = i
            target[n] = dest
            rank[n] = r
            ranks[dest] = r + 1
            info[dest, pl.ds(r, 1), :] = jnp.full((1, 128), slots[i].astype(jnp.float32))

        return n + goes.astype(jnp.int32)

    total = lax.fori_loop(0, count[0], sort, jnp.int32(0))
    tell = pltpu.make_async_copy(info, send.at[:, pl.ds(MOVE_CAP * ROWS, 8), :], info_sem)
    tell.start()
    for copy in base:
        copy.wait()
    cut_middle(windows)
    bring_maps.wait()

    def put(n):
        spot = send.at[target[n], pl.ds(pl.multiple_of(rank[n] * ROWS, ROWS), ROWS), :]
        return pltpu.make_async_copy(boxes.at[n], spot, put_sem.at[n])

    def chunk(at, carry):
        first = at * CHUNK
        here = jnp.minimum(total - first, CHUNK)

        def lay(j, c):
            i = order[first + j]
            bx = coords[0, i] - here_x * (CX // HALF)
            by = coords[1, i] - here_y * (CY // HALF)
            pack(windows, packed, j, bx, by)
            return c

        lax.fori_loop(0, here, lay, 0)
        grow(packed, maps, grown, 384)

        def step(j, c):
            n = first + j
            pltpu.make_async_copy(fine.at[order[n]], boxes.at[n], get_sem.at[n]).wait()

            @pl.when(fresh[order[n]] > 0)
            def _():
                fill_fresh(boxes, n, grown, j)

            for f in range(FIELDS):
                advance_field(boxes, n, grown, j, f)
            put(n).start()
            return c

        lax.fori_loop(0, here, step, 0)
        return carry

    lax.fori_loop(0, lax.div(total + CHUNK - 1, CHUNK), chunk, 0)

    def finish(n, c):
        put(n).wait()
        return c

    lax.fori_loop(0, total, finish, 0)
    tell.wait()


def home_kernel(
    count_in, coords_in, owner_in, slots_in, fresh_in, coarse, maps, mean, face, fine,
    fine_new, patchwork, covered,
    count, coords, owner, slots, fresh,
    windows, packed, grown, sums, ends, averaged, faced, boxes, table,
    int_sem, base_sem, get_sem, put_sem,
):
    here_x, here_y = lax.axis_index("gx"), lax.axis_index("gy")
    column = lax.axis_size("gy")
    base = base_copies(coarse, windows, base_sem)
    for copy in base:
        copy.start()
    fetch_all(
        [
            (count_in, count), (owner_in, owner), (slots_in, slots), (coords_in, coords),
            (fresh_in, fresh),
        ],
        int_sem,
    )
    total = count[0]
    across, along = CX // HALF, CY // HALF

    def clear(i, c):
        table[i] = 0
        return c

    lax.fori_loop(0, across * along, clear, 0)

    def local(i):
        return coords[0, i] - here_x * across, coords[1, i] - here_y * along

    def begin(i, c):
        pltpu.make_async_copy(fine.at[i], boxes.at[i], get_sem.at[i]).start()
        bx, by = local(i)
        table[bx * along + by] = 1
        return c

    lax.fori_loop(0, total, begin, 0)
    for copy in base:
        copy.wait()
    cut_middle(windows)

    def blank(step, c):
        at = pl.ds(pl.multiple_of(step * 16, 16), 16)
        for jb in range(2):
            covered[jb, at, :] = jnp.zeros((16, 128), jnp.float32)
            for f in range(FIELDS):
                for z in range(2):
                    patchwork[jb, f, z, at, :] = jnp.zeros((16, 128), jnp.float32)
        return c

    lax.fori_loop(0, CX // 16, blank, 0)

    def stays(i):
        return lax.div(owner[i], column) == here_x

    def chunk(step_at, carry):
        first = step_at * CHUNK
        here = jnp.minimum(total - first, CHUNK)

        def lay(j, c):
            bx, by = local(first + j)
            pack(windows, packed, j, bx, by)
            return c

        lax.fori_loop(0, here, lay, 0)
        grow(packed, maps, grown, 768)

        def step(j, c):
            n = first + j
            pltpu.make_async_copy(fine.at[n], boxes.at[n], get_sem.at[n]).wait()

            @pl.when(fresh[n] > 0)
            def _():
                fill_fresh(boxes, n, grown, j)

            at = pl.ds(pl.multiple_of(j * 16, 16), 16)
            for f in range(FIELDS):
                middle, final = advance_field(boxes, n, grown, j, f)
                split_store(
                    sums, f, at, jnp.concatenate([final[0] + final[1], final[2] + final[3]], axis=0)
                )
                split_store(
                    ends, f, at,
                    jnp.concatenate([middle[0] + middle[1], middle[2] + middle[3]], axis=0),
                )

            @pl.when(stays(n))
            def _():
                pltpu.make_async_copy(boxes.at[n], fine_new.at[slots[n]], put_sem.at[n]).start()

            return c

        lax.fori_loop(0, here, step, 0)
        for f in range(FIELDS):
            averaged[f] = jnp.dot(sums[f], mean[...], preferred_element_type=jnp.float32)
            faced[f] = jnp.dot(ends[f], face[f], preferred_element_type=jnp.float32)

        def settle(j, c):
            bx, by = local(first + j)
            jb = lax.div(by, 8)
            lane = lanes()
            window = lax.div(lane, 16) == lax.rem(by, 8)
            for part in range(2):
                at = pl.ds(pl.multiple_of(bx * HALF + 8 * part, 8), 8)
                covered[jb, at, :] = jnp.where(window, 1.0, covered[jb, at, :])
            for f in range(FIELDS):
                for z in range(2):
                    at = pl.ds(pl.multiple_of(j * 16 + 8 * z, 8), 8)
                    for xc in range(2):
                        rows = pl.ds(bx * HALF + xc, 8, stride=2)
                        patchwork[jb, f, z, rows, :] = jnp.where(
                            window,
                            averaged[f, at, 128 * xc : 128 * xc + 128],
                            patchwork[jb, f, z, rows, :],
                        )

            def x_side(high):
                row = bx * HALF + (HALF if high else -1)
                for f in range(FIELDS):
                    cx = COURANT[f][1]
                    sx = sign(cx)
                    weight = 2 * cx if high else -2 * cx
                    ghost = (sx > 0) != high
                    for z in range(2):
                        at = pl.ds(pl.multiple_of(j * 16 + 8 * z, 8), 8)
                        if ghost:
                            values = grown[f, at, 384:512]
                        else:
                            values = faced[f, at, 0:128]
                        line = values[7:8] if high else values[0:1]
                        old = patchwork[jb, f, z, pl.ds(row, 1), :]
                        patchwork[jb, f, z, pl.ds(row, 1), :] = old + jnp.where(
                            window[0:1], weight * line, 0.0
                        )

            def y_side(high):
                col = by * HALF + (HALF if high else -1)
                block = lax.div(col, 128)
                spot = lane == lax.rem(col, 128)
                for f in range(FIELDS):
                    cy = COURANT[f][2]
                    sy = sign(cy)
                    weight = 2 * cy if high else -2 * cy
                    ghost = (sy > 0) != high
                    for z in range(2):
                        at = pl.ds(pl.multiple_of(j * 16 + 8 * z, 8), 8)
                        for xc in range(2):
                            if ghost:
                                values = grown[f, at, 512 + 128 * xc : 640 + 128 * xc]
                            else:
                                values = faced[f, at, 128 + 128 * xc : 256 + 128 * xc]
                            rows = pl.ds(bx * HALF + xc, 8, stride=2)
                            old = patchwork[block, f, z, rows, :]
                            patchwork[block, f, z, rows, :] = old + jnp.where(
                                spot, weight * values, 0.0
                            )

            spot_at = bx * along + by
            pl.when(table[spot_at - along] == 0)(lambda: x_side(False))
            pl.when(table[spot_at + along] == 0)(lambda: x_side(True))
            pl.when(table[spot_at - 1] == 0)(lambda: y_side(False))
            pl.when(table[spot_at + 1] == 0)(lambda: y_side(True))
            return c

        lax.fori_loop(0, here, settle, 0)
        return carry

    lax.fori_loop(0, lax.div(total + CHUNK - 1, CHUNK), chunk, 0)

    def finish(n, c):
        @pl.when(stays(n))
        def _():
            pltpu.make_async_copy(boxes.at[n], fine_new.at[slots[n]], put_sem.at[n]).wait()

        return c

    lax.fori_loop(0, total, finish, 0)


def place_kernel(arrived, fine_part, fine_new, held, told, tell_sem, get_sem, put_sem):
    del fine_part
    tell = pltpu.make_async_copy(arrived.at[:, pl.ds(MOVE_CAP * ROWS, 8), :], told, tell_sem)
    tell.start()
    peers = arrived.shape[0]
    gets = [
        pltpu.make_async_copy(
            arrived.at[s, pl.ds(0, MOVE_CAP * ROWS), :], held.at[s], get_sem.at[s]
        )
        for s in range(peers)
    ]
    for get in gets:
        get.start()
    tell.wait()

    def put(s, r):
        slot = told[s, r, 0].astype(jnp.int32)
        copy = pltpu.make_async_copy(
            held.at[s, pl.ds(r * ROWS, ROWS), :],
            fine_new.at[jnp.maximum(slot, 0)],
            put_sem.at[s, r],
        )
        return slot >= 0, copy

    for s in range(peers):
        gets[s].wait()
        for r in range(MOVE_CAP):
            valid, copy = put(s, r)
            pl.when(valid)(copy.start)
    for s in range(peers):
        for r in range(MOVE_CAP):
            valid, copy = put(s, r)
            pl.when(valid)(copy.wait)


def base_kernel(coarse, rows, cols, patchwork, covered, coarse_new, held, mids):
    step = 32
    lane = lax.broadcasted_iota(jnp.int32, (step, CY), 1)
    full = jnp.concatenate([covered[0], covered[1]], axis=1)
    row_at = lax.broadcasted_iota(jnp.int32, (CX, CY), 0)
    lane_at = lax.broadcasted_iota(jnp.int32, (CX, CY), 1)
    below_x = jnp.where(row_at == 0, 0.0, pltpu.roll(full, 1, 0))
    above_x = jnp.where(row_at == CX - 1, 0.0, pltpu.roll(full, CX - 1, 0))
    below_y = jnp.where(lane_at == 0, 0.0, pltpu.roll(full, 1, 1))
    above_y = jnp.where(lane_at == CY - 1, 0.0, pltpu.roll(full, CY - 1, 1))
    for i, beside in enumerate((below_x, above_x, below_y, above_y)):
        mids[i] = 1.0 - beside
    mids[4] = 1.0 - full

    for f in range(FIELDS):
        cz, cx, cy = COURANT[f]
        sz, sx, sy = sign(cz), sign(cx), sign(cy)
        az, ax, ay = abs(cz), abs(cx), abs(cy)
        up_x, down_x = (0, 1) if sx > 0 else (1, 0)
        up_y, down_y = (2, 3) if sy > 0 else (3, 2)
        edge = 7 if sx > 0 else 8 + CX
        for z in range(2):
            held[0, z, 8 : 8 + CX, :] = coarse[f, z]
            held[0, z, edge : edge + 1, :] = rows[f, z, 0:1, :]
            held[1, z, edge : edge + 1, :] = rows[f, z, 1:2, :]

        def shifted(level, z, r):
            own = held[level, z, 8 + r : 8 + r + step, :]
            xs = held[level, z, 8 + r - sx : 8 + r - sx + step, :]
            col = cols[f, z, r : r + step, level : level + 1]
            if sy > 0:
                ys = jnp.where(lane == 0, col, pltpu.roll(own, 1, 1))
            else:
                ys = jnp.where(lane == CY - 1, col, pltpu.roll(own, CY - 1, 1))
            vz = held[level, (z - sz) % 2, 8 + r : 8 + r + step, :]
            return own, vz, xs, ys

        for z in range(2):
            for r in range(0, CX, step):
                own, vz, xs, ys = shifted(0, z, r)
                held[1, z, 8 + r : 8 + r + step, :] = own + 0.5 * (
                    az * (vz - own) + ax * (xs - own) + ay * (ys - own)
                )
        for z in range(2):
            for r in range(0, CX, step):
                own, vz, xs, ys = shifted(1, z, r)
                at = slice(r, r + step)
                value = held[0, z, 8 + r : 8 + r + step, :] + az * (vz - own)
                value += ax * (mids[up_x, at] * xs - mids[down_x, at] * own)
                value += ay * (mids[up_y, at] * ys - mids[down_y, at] * own)
                for jb in range(2):
                    cut = slice(128 * jb, 128 * jb + 128)
                    coarse_new[f, z, at, cut] = jnp.where(
                        mids[4, at, cut] > 0.5,
                        value[:, cut] + patchwork[jb, f, z, at, :],
                        patchwork[jb, f, z, at, :],
                    )


def shift_pairs(axis, forward):
    count = lax.axis_size(axis)
    step = 1 if forward else count - 1
    return [(i, (i + step) % count) for i in range(count)]


def upwind_edges(values, axis, signs, low, high):
    plus = [f for f in range(FIELDS) if signs[f] > 0]
    minus = [f for f in range(FIELDS) if signs[f] < 0]
    from_low = lax.ppermute(jnp.stack([high[f] for f in plus]), axis, shift_pairs(axis, True))
    from_high = lax.ppermute(jnp.stack([low[f] for f in minus]), axis, shift_pairs(axis, False))
    return jnp.stack(
        [
            from_low[plus.index(f)] if signs[f] > 0 else from_high[minus.index(f)]
            for f in range(FIELDS)
        ]
    )


def halos(coarse):
    sx = [sign(c[1]) for c in COURANT]
    sy = [sign(c[2]) for c in COURANT]
    near_far_low = coarse[:, :, 0:2, :]
    near_far_high = jnp.flip(coarse[:, :, -2:, :], axis=2)
    rows = upwind_edges(coarse, "gx", sx, near_far_low, near_far_high)
    near, far = rows[:, :, 0], rows[:, :, 1]

    def columns(low):
        cut = coarse[..., 0:2] if low else jnp.flip(coarse[..., -2:], axis=3)
        cut = jnp.swapaxes(cut, 2, 3)
        corner = near[..., 0] if low else near[..., -1]
        corner = jnp.broadcast_to(corner[:, :, None, None], cut.shape[:3] + (1,))
        return jnp.concatenate([cut, corner], axis=3)

    cols = upwind_edges(coarse, "gy", sy, columns(True), columns(False))
    near_col, far_col = cols[:, :, 0, :CX], cols[:, :, 1, :CX]
    corner = cols[:, :, 0, CX:]
    speed = jnp.abs(jnp.array(COURANT, jnp.float32))
    sz = [sign(c[0]) for c in COURANT]

    def beside(line, signs, edge):
        plus = jnp.concatenate([edge, line[..., :-1]], axis=2)
        minus = jnp.concatenate([line[..., 1:], edge], axis=2)
        return jnp.stack([plus[f] if signs[f] > 0 else minus[f] for f in range(FIELDS)])

    def half_step(line, across, along, across_at, along_at):
        up_z = jnp.stack([jnp.roll(line[f], sz[f], axis=0) for f in range(FIELDS)])
        return line + 0.5 * (
            speed[:, 0, None, None] * (up_z - line)
            + speed[:, across_at, None, None] * (across - line)
            + speed[:, along_at, None, None] * (along - line)
        )

    mid_row = half_step(near, far, beside(near, sy, corner), 1, 2)
    mid_col = half_step(near_col, far_col, beside(near_col, sx, corner), 2, 1)
    return (
        jnp.stack([near, mid_row], axis=2),
        jnp.swapaxes(jnp.stack([near_col, mid_col], axis=2), 2, 3),
    )


def per_device(coarse, fine_old, old_count, box_coords, new_owner, new_slot, fresh_box):
    peers = lax.axis_size("gx")
    fine = fine_old.reshape(OLD_CAP, FIELDS, BZ, 8, 128)
    fine = fine.transpose(0, 1, 3, 2, 4).reshape(OLD_CAP, ROWS, 128)
    vmem = pl.BlockSpec(memory_space=pltpu.VMEM)
    hbm = pl.BlockSpec(memory_space=pl.ANY)
    box = (ROWS, 128)
    rows = CHUNK * 16
    limit = pltpu.CompilerParams(vmem_limit_bytes=48 * 1024 * 1024)
    integers = (old_count, box_coords, new_owner, new_slot, fresh_box)
    held_integers = [pltpu.SMEM(values.shape, jnp.int32) for values in integers]

    send = pl.pallas_call(
        send_kernel,
        out_shape=jax.ShapeDtypeStruct((peers, MOVE_CAP * ROWS + 8, 128), jnp.float32),
        in_specs=[hbm] * 8,
        out_specs=hbm,
        scratch_shapes=held_integers
        + [
            pltpu.VMEM((FIELDS, 256, 384), jnp.bfloat16),
            pltpu.VMEM((3, FIELDS, 2, CX, 128), jnp.float32),
            pltpu.VMEM((FIELDS, rows, 256), jnp.bfloat16),
            pltpu.VMEM((FIELDS, rows, 384), jnp.float32),
            pltpu.VMEM((peers * MOVE_CAP,) + box, jnp.float32),
            pltpu.VMEM((peers, 8, 128), jnp.float32),
            pltpu.SMEM((OLD_CAP,), jnp.int32),
            pltpu.SMEM((OLD_CAP,), jnp.int32),
            pltpu.SMEM((OLD_CAP,), jnp.int32),
            pltpu.SMEM((peers,), jnp.int32),
            pltpu.SemaphoreType.DMA((5,)),
            pltpu.SemaphoreType.DMA((3,)),
            pltpu.SemaphoreType.DMA,
            pltpu.SemaphoreType.DMA,
            pltpu.SemaphoreType.DMA((peers * MOVE_CAP,)),
            pltpu.SemaphoreType.DMA((peers * MOVE_CAP,)),
        ],
        compiler_params=limit,
        cost_estimate=pl.CostEstimate(flops=10**8, bytes_accessed=8 * 10**6, transcendentals=0),
    )(*integers, coarse, jnp.asarray(np.ascontiguousarray(GROW[:, :, :384])), fine)
    arrived = lax.all_to_all(send, "gx", split_axis=0, concat_axis=0, tiled=True)
    later, _ = lax.optimization_barrier((coarse, send))

    fine_part, patchwork, covered = pl.pallas_call(
        home_kernel,
        out_shape=(
            jax.ShapeDtypeStruct((BOX_DEV,) + box, jnp.float32),
            jax.ShapeDtypeStruct((2, FIELDS, 2, CX, 128), jnp.float32),
            jax.ShapeDtypeStruct((2, CX, 128), jnp.float32),
        ),
        in_specs=[hbm] * 6 + [vmem] * 3 + [hbm],
        out_specs=(hbm, vmem, vmem),
        scratch_shapes=held_integers
        + [
            pltpu.VMEM((3, FIELDS, 2, CX, 128), jnp.float32),
            pltpu.VMEM((FIELDS, rows, 256), jnp.bfloat16),
            pltpu.VMEM((FIELDS, rows, 768), jnp.float32),
            pltpu.VMEM((FIELDS, rows, 256), jnp.bfloat16),
            pltpu.VMEM((FIELDS, rows, 256), jnp.bfloat16),
            pltpu.VMEM((FIELDS, rows, 256), jnp.float32),
            pltpu.VMEM((FIELDS, rows, 384), jnp.float32),
            pltpu.VMEM((OLD_CAP,) + box, jnp.float32),
            pltpu.SMEM(((CX // HALF) * (CY // HALF),), jnp.int32),
            pltpu.SemaphoreType.DMA((5,)),
            pltpu.SemaphoreType.DMA((3,)),
            pltpu.SemaphoreType.DMA((OLD_CAP,)),
            pltpu.SemaphoreType.DMA((OLD_CAP,)),
        ],
        compiler_params=limit,
        cost_estimate=pl.CostEstimate(flops=10**9, bytes_accessed=60 * 10**6, transcendentals=0),
    )(*integers, later, jnp.asarray(GROW), jnp.asarray(MEAN), jnp.asarray(FACE), fine)

    edge_rows, edge_cols = halos(later)
    coarse_new = pl.pallas_call(
        base_kernel,
        out_shape=jax.ShapeDtypeStruct(coarse.shape, coarse.dtype),
        in_specs=[vmem] * 5,
        out_specs=vmem,
        scratch_shapes=[
            pltpu.VMEM((2, 2, CX + 16, CY), jnp.float32),
            pltpu.VMEM((5, CX, CY), jnp.float32),
        ],
        compiler_params=limit,
        cost_estimate=pl.CostEstimate(flops=10**8, bytes_accessed=20 * 10**6, transcendentals=0),
    )(later, edge_rows, edge_cols, patchwork, covered)

    fine_new = pl.pallas_call(
        place_kernel,
        out_shape=jax.ShapeDtypeStruct((BOX_DEV,) + box, jnp.float32),
        in_specs=[hbm, hbm],
        out_specs=hbm,
        scratch_shapes=[
            pltpu.VMEM((peers, MOVE_CAP * ROWS, 128), jnp.float32),
            pltpu.SMEM((peers, 8, 128), jnp.float32),
            pltpu.SemaphoreType.DMA,
            pltpu.SemaphoreType.DMA((peers,)),
            pltpu.SemaphoreType.DMA((peers, MOVE_CAP)),
        ],
        input_output_aliases={1: 0},
        compiler_params=limit,
        cost_estimate=pl.CostEstimate(flops=0, bytes_accessed=5 * 10**6, transcendentals=0),
    )(arrived, fine_part)
    fine_new = fine_new.reshape(BOX_DEV, FIELDS, 8, BZ, 128).transpose(0, 1, 3, 2, 4)
    return coarse_new, fine_new.reshape(BOX_DEV, FIELDS, BZ, BX * BX)


def solution(mesh):
    return jax.shard_map(
        per_device,
        mesh=mesh,
        in_specs=(
            P(None, None, "gx", "gy"),
            P(("gx", "gy"), None, None, None),
            P(("gx", "gy")),
            P(None, ("gx", "gy")),
            P(("gx", "gy")),
            P(("gx", "gy")),
            P(("gx", "gy")),
        ),
        out_specs=(P(None, None, "gx", "gy"), P(("gx", "gy"), None, None, None)),
        check_vma=False,
    )
```

```python
import jax
import jax.numpy as jnp
import numpy as np
import ml_dtypes
from jax import lax
from jax.experimental import pallas as pl
from jax.experimental.pallas import tpu as pltpu
from jax.sharding import PartitionSpec as P

BX = 32
BZ = 4
HALF = 16
BOX_DEV = 32
MOVE_CAP = 2
FIELDS = 5
CHUNK = 8

COURANT = (
    (0.1, 0.2, -0.12),
    (-0.08, -0.15, 0.2),
    (0.12, 0.1, 0.18),
    (-0.05, 0.22, -0.15),
    (0.15, -0.18, -0.1),
)
CX, CY, OLD_CAP = 128, 256, 62
ROWS = FIELDS * BX


def sign(value):
    return 1 if value > 0 else -1


def first_row(sx):
    return -2 if sx > 0 else -1


def patch_maps(sx, sy):
    maps = np.zeros((128, 6, 128), np.float32)
    start = first_row(sx)

    def put(block, lane, row, col, value):
        maps[(row - start) * 20 + col, block, lane] += value

    def child(block, lane, row, col, b, e):
        put(block, lane, row, col, 1.0)
        if b:
            put(block, lane, row + 1, col, b / 8)
            put(block, lane, row - 1, col, -b / 8)
        if e:
            put(block, lane, row, col + 1, e / 8)
            put(block, lane, row, col - 1, -e / 8)

    for lane in range(128):
        xg, y = divmod(lane, 32)
        b = 1 if xg % 2 else -1
        e = 1 if y % 2 else -1
        child(0, lane, xg // 2, 2 + y // 2, b, e)
        if sx > 0 and xg == 0:
            child(1, lane, -1, 2 + y // 2, 1, e)
        if sx < 0 and xg == 3:
            child(1, lane, 2, 2 + y // 2, -1, e)
        if sy > 0 and y == 0:
            child(2, lane, xg // 2, 1, b, 1)
        if sy < 0 and y == 31:
            child(2, lane, xg // 2, 18, b, -1)
        child(3, lane, -1 if sx > 0 else 2, 2 + lane % 16, sx, 0)
        for xc in range(2):
            child(4 + xc, lane, xc, 1 if sy > 0 else 18, 0, sy)
    flat = maps.reshape(128, 768)
    return np.concatenate([flat, flat])


def mean_map():
    maps = np.zeros((128, 2, 128), np.float32)
    for source in range(128):
        xg, y = divmod(source, 32)
        for lane in range(128):
            if lane % 16 == y // 2:
                maps[source, xg // 2, lane] = 0.125
    flat = maps.reshape(128, 256)
    return np.concatenate([flat, flat])


def face_map(sx, sy):
    maps = np.zeros((128, 3, 128), np.float32)
    for source in range(128):
        xg, y = divmod(source, 32)
        for lane in range(128):
            if xg == (3 if sx > 0 else 0) and lane % 16 == y // 2:
                maps[source, 0, lane] = 0.25
            if y == (31 if sy > 0 else 0):
                maps[source, 1 + xg // 2, lane] = 0.25
    flat = maps.reshape(128, 384)
    return np.concatenate([flat, flat])


def all_maps():
    grow = np.stack([patch_maps(sign(c[1]), sign(c[2])) for c in COURANT])
    face = np.stack([face_map(sign(c[1]), sign(c[2])) for c in COURANT])
    half = ml_dtypes.bfloat16
    return grow.astype(half), mean_map().astype(half), face.astype(half)


GROW, MEAN, FACE = all_maps()


def lanes():
    return lax.broadcasted_iota(jnp.int32, (8, 128), 1)


def sublanes():
    return lax.broadcasted_iota(jnp.int32, (8, 128), 0)


def base_copies(coarse, windows, sem):
    return [
        pltpu.make_async_copy(coarse.at[:, :, :, pl.ds(64 * w, 128)], windows.at[w], sem.at[w])
        for w in (0, 2)
    ]


def cut_middle(windows):
    def rows(step, carry):
        at = pl.ds(pl.multiple_of(step * 16, 16), 16)
        lane = lax.broadcasted_iota(jnp.int32, (16, 128), 1)
        for f in range(FIELDS):
            for z in range(2):
                both = jnp.where(lane < 64, windows[2, f, z, at, :], windows[0, f, z, at, :])
                windows[1, f, z, at, :] = pltpu.roll(both, 64, 1)
        return carry

    lax.fori_loop(0, CX // 16, rows, 0)


def split_store(target, f, at, value):
    high = value.astype(jnp.bfloat16)
    target[f, at, 0:128] = high
    target[f, at, 128:256] = (value - high.astype(jnp.float32)).astype(jnp.bfloat16)


def pack(windows, packed, j, bx, by):
    which = (by >= 7).astype(jnp.int32) + (by >= 9).astype(jnp.int32)
    start = by * HALF - 2 - which * 64
    lane = lanes()
    shifts = [lax.rem(20 * i - start + 256, 128) for i in range(5)]
    for f in range(FIELDS):
        first = first_row(sign(COURANT[f][1]))
        both = []
        for z in range(2):
            held = None
            for i in range(5):
                row = windows[which, f, z, pl.ds(bx * HALF + first + i, 8, stride=2), :]
                row = pltpu.roll(row, shifts[i], 1)
                held = row if held is None else jnp.where(lane < 20 * i, held, row)
            both.append(held)
        at = pl.ds(pl.multiple_of(j * 16, 16), 16)
        split_store(packed, f, at, jnp.concatenate(both, axis=0))


def z_children(values):
    count = len(values)
    out = []
    for z in range(count):
        tilt = 0.125 * (values[(z + 1) % count] - values[(z - 1) % count])
        out += [values[z] - tilt, values[z] + tilt]
    return out


def box_rows(f, z):
    return pl.ds(32 * f + z, 8, stride=4)


def fill_fresh(box, grown, j):
    for f in range(FIELDS):
        parts = [grown[f, pl.ds(pl.multiple_of(j * 16 + 8 * z, 8), 8), 0:128] for z in range(2)]
        for z, value in enumerate(z_children(parts)):
            box[box_rows(f, z), :] = value


def upwind(values, sx, sy, sz, lane):
    out = []
    for z in range(BZ):
        v = values[z]
        vz = values[(z - sz) % BZ]
        if sx > 0:
            near = pltpu.roll(v, 32, 1)
            xs = jnp.where(lane < 32, pltpu.roll(near, 1, 0), near)
        else:
            near = pltpu.roll(v, 96, 1)
            xs = jnp.where(lane >= 96, pltpu.roll(near, 7, 0), near)
        ys = pltpu.roll(v, 1 if sy > 0 else 127, 1)
        out.append((vz, xs, ys))
    return out


def advance_field(box, out, out_at, grown, j, f):
    cz, cx, cy = COURANT[f]
    sz, sx, sy = sign(cz), sign(cx), sign(cy)
    az, ax, ay = 2 * abs(cz), 2 * abs(cx), 2 * abs(cy)
    total = az + ax + ay
    lane, sub = lanes(), sublanes()
    edge_x = ((sub == 0) & (lane < 32)) if sx > 0 else ((sub == 7) & (lane >= 96))
    edge_y = (lane % 32) == (0 if sy > 0 else 31)
    ghost_x = jnp.where(edge_x, ax, 0.0)
    gain_x = jnp.where(edge_x, 0.0, ax)
    gain_y = jnp.where(edge_y, 0.0, ay)
    rims = []
    for z in range(2):
        at = pl.ds(pl.multiple_of(j * 16 + 8 * z, 8), 8)
        rims.append(ghost_x * grown[f, at, 128:256] + ay * grown[f, at, 256:384])
    rims = z_children(rims)
    state = [box[box_rows(f, z), :] for z in range(BZ)]
    middle = []
    half_x, half_y = 0.5 * gain_x, 0.5 * gain_y
    for z, (vz, xs, ys) in enumerate(upwind(state, sx, sy, sz, lane)):
        middle.append(
            (1 - 0.5 * total) * state[z]
            + (0.5 * az) * vz
            + half_x * xs
            + half_y * ys
            + 0.5 * rims[z]
        )
    final = []
    for z, (vz, xs, ys) in enumerate(upwind(middle, sx, sy, sz, lane)):
        final.append(
            (state[z] + rims[z]) - total * middle[z] + az * vz + gain_x * xs + gain_y * ys
        )
    for z in range(BZ):
        out[pl.ds(out_at + 32 * f + z, 8, stride=4), :] = final[z]
    return middle, final


def grow(packed, maps, grown, width):
    for f in range(FIELDS):
        grown[f, :, 0:width] = jnp.dot(
            packed[f], maps[f][:, 0:width], preferred_element_type=jnp.float32
        )


def int_copies(pairs, sem):
    return [
        pltpu.make_async_copy(source, target, sem.at[i]) for i, (source, target) in enumerate(pairs)
    ]


FINE_PARTS = ((0, 16), (16, 16), (32, 16), (48, OLD_CAP - 48))
GROUP = CHUNK // MOVE_CAP


def fine_copies(fine, boxes, sem):
    return [
        pltpu.make_async_copy(fine.at[pl.ds(at, n)], boxes.at[pl.ds(at, n)], sem.at[i])
        for i, (at, n) in enumerate(FINE_PARTS)
    ]


def send_kernel(
    count_in, coords_in, owner_in, slots_in, fresh_in, coarse, maps_in, fine, send,
    count, coords, owner, slots, fresh, maps,
    windows, packed, grown, boxes, outgoing, order, ranks,
    int_sem, base_sem, map_sem, get_sem, put_sem,
):
    here_x, here_y = lax.axis_index("gx"), lax.axis_index("gy")
    column = lax.axis_size("gy")
    ints = int_copies(
        [
            (count_in, count), (owner_in, owner), (slots_in, slots), (coords_in, coords),
            (fresh_in, fresh),
        ],
        int_sem,
    )
    base = base_copies(coarse, windows, base_sem)
    bring_maps = pltpu.make_async_copy(maps_in, maps, map_sem)
    gets = fine_copies(fine, boxes, get_sem)
    for copy in ints + base + [bring_maps] + gets:
        copy.start()
    peers = outgoing.shape[0]
    for i in range(peers):
        ranks[i] = 0
        outgoing[i, pl.ds(MOVE_CAP * ROWS, 8), :] = jnp.full((8, 128), -1.0, jnp.float32)
    for i in range(peers * MOVE_CAP):
        order[i] = -1
    for copy in ints:
        copy.wait()

    def sort(i, c):
        dest = lax.div(owner[i], column)

        @pl.when(dest != here_x)
        def _():
            r = ranks[dest]
            order[dest * MOVE_CAP + r] = i
            ranks[dest] = r + 1
            outgoing[dest, pl.ds(MOVE_CAP * ROWS + r, 1), :] = jnp.full(
                (1, 128), slots[i].astype(jnp.float32)
            )

        return c

    lax.fori_loop(0, count[0], sort, 0)
    for copy in base:
        copy.wait()
    cut_middle(windows)
    bring_maps.wait()
    puts = []
    for group in range(peers // GROUP):
        first = group * CHUNK

        def lay(j, c):
            i = order[first + j]

            @pl.when(i >= 0)
            def _():
                bx = coords[0, i] - here_x * (CX // HALF)
                by = coords[1, i] - here_y * (CY // HALF)
                pack(windows, packed, j, bx, by)

            return c

        lax.fori_loop(0, CHUNK, lay, 0)
        grow(packed, maps, grown, 384)
        if group == 0:
            for copy in gets:
                copy.wait()

        def step(j, c):
            i = order[first + j]

            @pl.when(i >= 0)
            def _():
                box = boxes.at[i]
                pl.when(fresh[i] > 0)(lambda: fill_fresh(box, grown, j))
                out = outgoing.at[group * GROUP + lax.div(j, MOVE_CAP)]
                out_at = lax.rem(j, MOVE_CAP) * ROWS
                for f in range(FIELDS):
                    advance_field(box, out, out_at, grown, j, f)

            return c

        lax.fori_loop(0, CHUNK, step, 0)
        part = pl.ds(group * GROUP, GROUP)
        puts.append(pltpu.make_async_copy(outgoing.at[part], send.at[part], put_sem.at[group]))
        puts[-1].start()
    for put in puts:
        put.wait()


def home_kernel(
    count_in, coords_in, owner_in, slots_in, fresh_in, coarse, maps_in, mean_in, face_in, fine,
    fine_new, patchwork, covered,
    count, coords, owner, slots, fresh, maps, mean, face,
    windows, packed, grown, sums, ends, averaged, faced, boxes, kept, table,
    int_sem, base_sem, map_sem, get_sem, put_sem,
):
    here_x, here_y = lax.axis_index("gx"), lax.axis_index("gy")
    column = lax.axis_size("gy")
    ints = int_copies(
        [
            (count_in, count), (owner_in, owner), (slots_in, slots), (coords_in, coords),
            (fresh_in, fresh),
        ],
        int_sem,
    )
    base = base_copies(coarse, windows, base_sem)
    bring = int_copies([(maps_in, maps), (mean_in, mean), (face_in, face)], map_sem)
    gets = fine_copies(fine, boxes, get_sem)
    for copy in ints + base + bring + gets:
        copy.start()
    for copy in ints:
        copy.wait()
    total = count[0]
    across, along = CX // HALF, CY // HALF

    def clear(i, c):
        table[i] = 0
        return c

    lax.fori_loop(0, across * along, clear, 0)

    def local(i):
        return coords[0, i] - here_x * across, coords[1, i] - here_y * along

    def begin(i, c):
        bx, by = local(i)
        table[bx * along + by] = 1
        return c

    lax.fori_loop(0, total, begin, 0)
    for copy in base:
        copy.wait()
    cut_middle(windows)

    def blank(step, c):
        at = pl.ds(pl.multiple_of(step * 16, 16), 16)
        for jb in range(2):
            covered[jb, at, :] = jnp.zeros((16, 128), jnp.float32)
            for f in range(FIELDS):
                for z in range(2):
                    patchwork[jb, f, z, at, :] = jnp.zeros((16, 128), jnp.float32)
        return c

    lax.fori_loop(0, CX // 16, blank, 0)

    for copy in bring + gets:
        copy.wait()

    def stays(i):
        return lax.div(owner[i], column) == here_x

    def chunk(step_at, carry):
        first = step_at * CHUNK
        here = jnp.minimum(total - first, CHUNK)

        def lay(j, c):
            bx, by = local(first + j)
            pack(windows, packed, j, bx, by)
            return c

        lax.fori_loop(0, here, lay, 0)
        grow(packed, maps, grown, 768)

        def step(j, c):
            n = first + j
            box = boxes.at[n]
            pl.when(fresh[n] > 0)(lambda: fill_fresh(box, grown, j))
            out = kept.at[jnp.where(stays(n), slots[n], BOX_DEV)]
            at = pl.ds(pl.multiple_of(j * 16, 16), 16)
            for f in range(FIELDS):
                middle, final = advance_field(box, out, 0, grown, j, f)
                split_store(
                    sums, f, at, jnp.concatenate([final[0] + final[1], final[2] + final[3]], axis=0)
                )
                split_store(
                    ends, f, at,
                    jnp.concatenate([middle[0] + middle[1], middle[2] + middle[3]], axis=0),
                )

            return c

        lax.fori_loop(0, here, step, 0)
        for f in range(FIELDS):
            averaged[f] = jnp.dot(sums[f], mean[...], preferred_element_type=jnp.float32)
            faced[f] = jnp.dot(ends[f], face[f], preferred_element_type=jnp.float32)

        def settle(j, c):
            bx, by = local(first + j)
            jb = lax.div(by, 8)
            lane = lanes()
            window = lax.div(lane, 16) == lax.rem(by, 8)
            for part in range(2):
                at = pl.ds(pl.multiple_of(bx * HALF + 8 * part, 8), 8)
                covered[jb, at, :] = jnp.where(window, 1.0, covered[jb, at, :])
            for f in range(FIELDS):
                for z in range(2):
                    at = pl.ds(pl.multiple_of(j * 16 + 8 * z, 8), 8)
                    for xc in range(2):
                        rows = pl.ds(bx * HALF + xc, 8, stride=2)
                        patchwork[jb, f, z, rows, :] = jnp.where(
                            window,
                            averaged[f, at, 128 * xc : 128 * xc + 128],
                            patchwork[jb, f, z, rows, :],
                        )

            def x_side(high):
                row = bx * HALF + (HALF if high else -1)
                for f in range(FIELDS):
                    cx = COURANT[f][1]
                    sx = sign(cx)
                    weight = 2 * cx if high else -2 * cx
                    ghost = (sx > 0) != high
                    for z in range(2):
                        at = pl.ds(pl.multiple_of(j * 16 + 8 * z, 8), 8)
                        if ghost:
                            values = grown[f, at, 384:512]
                        else:
                            values = faced[f, at, 0:128]
                        line = values[7:8] if high else values[0:1]
                        old = patchwork[jb, f, z, pl.ds(row, 1), :]
                        patchwork[jb, f, z, pl.ds(row, 1), :] = old + jnp.where(
                            window[0:1], weight * line, 0.0
                        )

            def y_side(high):
                col = by * HALF + (HALF if high else -1)
                block = lax.div(col, 128)
                spot = lane == lax.rem(col, 128)
                for f in range(FIELDS):
                    cy = COURANT[f][2]
                    sy = sign(cy)
                    weight = 2 * cy if high else -2 * cy
                    ghost = (sy > 0) != high
                    for z in range(2):
                        at = pl.ds(pl.multiple_of(j * 16 + 8 * z, 8), 8)
                        for xc in range(2):
                            if ghost:
                                values = grown[f, at, 512 + 128 * xc : 640 + 128 * xc]
                            else:
                                values = faced[f, at, 128 + 128 * xc : 256 + 128 * xc]
                            rows = pl.ds(bx * HALF + xc, 8, stride=2)
                            old = patchwork[block, f, z, rows, :]
                            patchwork[block, f, z, rows, :] = old + jnp.where(
                                spot, weight * values, 0.0
                            )

            spot_at = bx * along + by
            pl.when(table[spot_at - along] == 0)(lambda: x_side(False))
            pl.when(table[spot_at + along] == 0)(lambda: x_side(True))
            pl.when(table[spot_at - 1] == 0)(lambda: y_side(False))
            pl.when(table[spot_at + 1] == 0)(lambda: y_side(True))
            return c

        lax.fori_loop(0, here, settle, 0)
        return carry

    lax.fori_loop(0, lax.div(total + CHUNK - 1, CHUNK), chunk, 0)

    put = pltpu.make_async_copy(kept.at[pl.ds(0, BOX_DEV)], fine_new, put_sem)
    put.start()
    put.wait()


def place_kernel(arrived, fine_part, fine_new, held, told, tell_sem, get_sem, put_sem):
    del fine_part
    tell = pltpu.make_async_copy(arrived.at[:, pl.ds(MOVE_CAP * ROWS, 8), :], told, tell_sem)
    tell.start()
    peers = arrived.shape[0]
    gets = [
        pltpu.make_async_copy(
            arrived.at[s, pl.ds(0, MOVE_CAP * ROWS), :], held.at[s], get_sem.at[s]
        )
        for s in range(peers)
    ]
    for get in gets:
        get.start()
    tell.wait()

    def put(s, r):
        slot = told[s, r, 0].astype(jnp.int32)
        copy = pltpu.make_async_copy(
            held.at[s, pl.ds(r * ROWS, ROWS), :],
            fine_new.at[jnp.maximum(slot, 0)],
            put_sem.at[s, r],
        )
        return slot >= 0, copy

    for s in range(peers):
        gets[s].wait()
        for r in range(MOVE_CAP):
            valid, copy = put(s, r)
            pl.when(valid)(copy.start)
    for s in range(peers):
        for r in range(MOVE_CAP):
            valid, copy = put(s, r)
            pl.when(valid)(copy.wait)


PLUS_X = [f for f in range(FIELDS) if COURANT[f][1] > 0]
MINUS_X = [f for f in range(FIELDS) if COURANT[f][1] < 0]
PLUS_Y = [f for f in range(FIELDS) if COURANT[f][2] > 0]
MINUS_Y = [f for f in range(FIELDS) if COURANT[f][2] < 0]


def edge_kernel(coarse, rows_plus, rows_minus, cols_plus, cols_minus):
    for at, f in enumerate(PLUS_X):
        rows_plus[at] = coarse[f, :, CX - 8 :, :]
    for at, f in enumerate(MINUS_X):
        rows_minus[at] = coarse[f, :, 0:8, :]
    for z in range(2):
        for at, f in enumerate(PLUS_Y):
            cols_plus[at, z] = jnp.transpose(coarse[f, z, :, CY - 128 :])[120:128]
        for at, f in enumerate(MINUS_Y):
            cols_minus[at, z] = jnp.transpose(coarse[f, z, :, 0:128])[0:8]


def upwind_columns(cols_plus, cols_minus, f):
    if COURANT[f][2] > 0:
        return cols_plus[PLUS_Y.index(f)]
    return cols_minus[MINUS_Y.index(f)]


def join_kernel(rows_plus, rows_minus, cols_plus, cols_minus, send_plus, send_minus):
    for fields, rows, out in (
        (PLUS_X, rows_plus, send_plus), (MINUS_X, rows_minus, send_minus),
    ):
        for at, f in enumerate(fields):
            out[at, :, :, 0:CY] = rows[at]
            out[at, :, :, CY : CY + CX] = upwind_columns(cols_plus, cols_minus, f)


def base_kernel(
    coarse, rows_plus, rows_minus, cols_plus, cols_minus, patchwork, covered, coarse_new,
    held, mids, turned,
):
    step = 32
    lane = lax.broadcasted_iota(jnp.int32, (step, CY), 1)
    full = jnp.concatenate([covered[0], covered[1]], axis=1)
    row_at = lax.broadcasted_iota(jnp.int32, (CX, CY), 0)
    lane_at = lax.broadcasted_iota(jnp.int32, (CX, CY), 1)
    below_x = jnp.where(row_at == 0, 0.0, pltpu.roll(full, 1, 0))
    above_x = jnp.where(row_at == CX - 1, 0.0, pltpu.roll(full, CX - 1, 0))
    below_y = jnp.where(lane_at == 0, 0.0, pltpu.roll(full, 1, 1))
    above_y = jnp.where(lane_at == CY - 1, 0.0, pltpu.roll(full, CY - 1, 1))
    for i, beside in enumerate((below_x, above_x, below_y, above_y)):
        mids[i] = 1.0 - beside
    mids[4] = 1.0 - full

    for f in range(FIELDS):
        cz, cx, cy = COURANT[f]
        sz, sx, sy = sign(cz), sign(cx), sign(cy)
        az, ax, ay = abs(cz), abs(cx), abs(cy)
        up_x, down_x = (0, 1) if sx > 0 else (1, 0)
        up_y, down_y = (2, 3) if sy > 0 else (3, 2)
        near_x, near_y = (7 if sx > 0 else 0), (7 if sy > 0 else 0)
        halo = rows_plus[PLUS_X.index(f)] if sx > 0 else rows_minus[MINUS_X.index(f)]
        row_slabs = [halo[z][:, 0:CY] for z in range(2)]
        columns = upwind_columns(cols_plus, cols_minus, f)
        col_slabs = [columns[z] for z in range(2)]
        corner_lane = CY + (CX - 1 if sx > 0 else 0)
        edge = 7 if sx > 0 else 8 + CX
        lane_row = lax.broadcasted_iota(jnp.int32, (8, CY), 1)
        lane_col = lax.broadcasted_iota(jnp.int32, (8, CX), 1)
        for z in range(2):
            spot = halo[z][near_y : near_y + 1, corner_lane : corner_lane + 1]
            row, col = row_slabs[z], col_slabs[z]
            far = pltpu.roll(row, 1 if sx > 0 else 7, 0)
            if sy > 0:
                along = jnp.where(lane_row == 0, spot, pltpu.roll(row, 1, 1))
            else:
                along = jnp.where(lane_row == CY - 1, spot, pltpu.roll(row, CY - 1, 1))
            mid_row = row + 0.5 * (
                az * (row_slabs[(z - sz) % 2] - row) + ax * (far - row) + ay * (along - row)
            )
            far = pltpu.roll(col, 1 if sy > 0 else 7, 0)
            if sx > 0:
                along = jnp.where(lane_col == 0, spot, pltpu.roll(col, 1, 1))
            else:
                along = jnp.where(lane_col == CX - 1, spot, pltpu.roll(col, CX - 1, 1))
            mid_col = col + 0.5 * (
                az * (col_slabs[(z - sz) % 2] - col) + ay * (far - col) + ax * (along - col)
            )
            held[0, z, 8 : 8 + CX, :] = coarse[f, z]
            held[0, z, edge : edge + 1, :] = row[near_x : near_x + 1]
            held[1, z, edge : edge + 1, :] = mid_row[near_x : near_x + 1]
            turned[z] = jnp.transpose(
                jnp.concatenate([col, mid_col, jnp.zeros((112, CX), jnp.float32)], axis=0)
            )

        def shifted(level, z, r):
            own = held[level, z, 8 + r : 8 + r + step, :]
            xs = held[level, z, 8 + r - sx : 8 + r - sx + step, :]
            col = turned[z, r : r + step, 8 * level + near_y : 8 * level + near_y + 1]
            if sy > 0:
                ys = jnp.where(lane == 0, col, pltpu.roll(own, 1, 1))
            else:
                ys = jnp.where(lane == CY - 1, col, pltpu.roll(own, CY - 1, 1))
            vz = held[level, (z - sz) % 2, 8 + r : 8 + r + step, :]
            return own, vz, xs, ys

        for z in range(2):
            for r in range(0, CX, step):
                own, vz, xs, ys = shifted(0, z, r)
                held[1, z, 8 + r : 8 + r + step, :] = own + 0.5 * (
                    az * (vz - own) + ax * (xs - own) + ay * (ys - own)
                )
        for z in range(2):
            for r in range(0, CX, step):
                own, vz, xs, ys = shifted(1, z, r)
                at = slice(r, r + step)
                value = held[0, z, 8 + r : 8 + r + step, :] + az * (vz - own)
                value += ax * (mids[up_x, at] * xs - mids[down_x, at] * own)
                value += ay * (mids[up_y, at] * ys - mids[down_y, at] * own)
                for jb in range(2):
                    cut = slice(128 * jb, 128 * jb + 128)
                    coarse_new[f, z, at, cut] = jnp.where(
                        mids[4, at, cut] > 0.5,
                        value[:, cut] + patchwork[jb, f, z, at, :],
                        patchwork[jb, f, z, at, :],
                    )


def pass_on(values, axis, step):
    count = lax.axis_size(axis)
    return lax.ppermute(values, axis, [(i, (i + step) % count) for i in range(count)])


def small_call(kernel, shapes, operands, limit):
    vmem = pl.BlockSpec(memory_space=pltpu.VMEM)
    return pl.pallas_call(
        kernel,
        out_shape=tuple(jax.ShapeDtypeStruct(shape, jnp.float32) for shape in shapes),
        in_specs=[vmem] * len(operands),
        out_specs=(vmem,) * len(shapes),
        compiler_params=limit,
        cost_estimate=pl.CostEstimate(flops=10**6, bytes_accessed=3 * 10**6, transcendentals=0),
    )(*operands)


def per_device(coarse, fine_old, old_count, box_coords, new_owner, new_slot, fresh_box):
    peers = lax.axis_size("gx")
    fine = fine_old.reshape(OLD_CAP, FIELDS, BZ, 8, 128)
    fine = fine.transpose(0, 1, 3, 2, 4).reshape(OLD_CAP, ROWS, 128)
    vmem = pl.BlockSpec(memory_space=pltpu.VMEM)
    hbm = pl.BlockSpec(memory_space=pltpu.HBM)
    box = (ROWS, 128)
    rows = CHUNK * 16
    limit = pltpu.CompilerParams(vmem_limit_bytes=60 * 1024 * 1024)
    integers = (old_count, box_coords, new_owner, new_slot, fresh_box)
    held_integers = [pltpu.SMEM(values.shape, jnp.int32) for values in integers]

    send = pl.pallas_call(
        send_kernel,
        out_shape=jax.ShapeDtypeStruct((peers, MOVE_CAP * ROWS + 8, 128), jnp.float32),
        in_specs=[hbm] * 8,
        out_specs=hbm,
        scratch_shapes=held_integers
        + [
            pltpu.VMEM((FIELDS, 256, 384), jnp.bfloat16),
            pltpu.VMEM((3, FIELDS, 2, CX, 128), jnp.float32),
            pltpu.VMEM((FIELDS, rows, 256), jnp.bfloat16),
            pltpu.VMEM((FIELDS, rows, 384), jnp.float32),
            pltpu.VMEM((OLD_CAP,) + box, jnp.float32),
            pltpu.VMEM((peers, MOVE_CAP * ROWS + 8, 128), jnp.float32),
            pltpu.SMEM((peers * MOVE_CAP,), jnp.int32),
            pltpu.SMEM((peers,), jnp.int32),
            pltpu.SemaphoreType.DMA((5,)),
            pltpu.SemaphoreType.DMA((3,)),
            pltpu.SemaphoreType.DMA,
            pltpu.SemaphoreType.DMA((4,)),
            pltpu.SemaphoreType.DMA((peers // GROUP,)),
        ],
        compiler_params=limit,
        cost_estimate=pl.CostEstimate(flops=10**8, bytes_accessed=8 * 10**6, transcendentals=0),
    )(*integers, coarse, jnp.asarray(np.ascontiguousarray(GROW[:, :, :384])), fine)
    arrived = lax.all_to_all(send, "gx", split_axis=0, concat_axis=0, tiled=True)
    later, _ = lax.optimization_barrier((coarse, send))

    rows_plus, rows_minus, cols_plus, cols_minus = small_call(
        edge_kernel,
        [
            (len(PLUS_X), 2, 8, CY), (len(MINUS_X), 2, 8, CY),
            (len(PLUS_Y), 2, 8, CX), (len(MINUS_Y), 2, 8, CX),
        ],
        [later],
        limit,
    )
    cols_plus = pass_on(cols_plus, "gy", 1)
    cols_minus = pass_on(cols_minus, "gy", -1)

    fine_part, patchwork, covered = pl.pallas_call(
        home_kernel,
        out_shape=(
            jax.ShapeDtypeStruct((BOX_DEV,) + box, jnp.float32),
            jax.ShapeDtypeStruct((2, FIELDS, 2, CX, 128), jnp.float32),
            jax.ShapeDtypeStruct((2, CX, 128), jnp.float32),
        ),
        in_specs=[hbm] * 10,
        out_specs=(hbm, vmem, vmem),
        scratch_shapes=held_integers
        + [
            pltpu.VMEM((FIELDS, 256, 768), jnp.bfloat16),
            pltpu.VMEM((256, 256), jnp.bfloat16),
            pltpu.VMEM((FIELDS, 256, 384), jnp.bfloat16),
            pltpu.VMEM((3, FIELDS, 2, CX, 128), jnp.float32),
            pltpu.VMEM((FIELDS, rows, 256), jnp.bfloat16),
            pltpu.VMEM((FIELDS, rows, 768), jnp.float32),
            pltpu.VMEM((FIELDS, rows, 256), jnp.bfloat16),
            pltpu.VMEM((FIELDS, rows, 256), jnp.bfloat16),
            pltpu.VMEM((FIELDS, rows, 256), jnp.float32),
            pltpu.VMEM((FIELDS, rows, 384), jnp.float32),
            pltpu.VMEM((OLD_CAP,) + box, jnp.float32),
            pltpu.VMEM((BOX_DEV + 1,) + box, jnp.float32),
            pltpu.SMEM(((CX // HALF) * (CY // HALF),), jnp.int32),
            pltpu.SemaphoreType.DMA((5,)),
            pltpu.SemaphoreType.DMA((3,)),
            pltpu.SemaphoreType.DMA((3,)),
            pltpu.SemaphoreType.DMA((4,)),
            pltpu.SemaphoreType.DMA,
        ],
        compiler_params=limit,
        cost_estimate=pl.CostEstimate(flops=10**9, bytes_accessed=60 * 10**6, transcendentals=0),
    )(*integers, later, jnp.asarray(GROW), jnp.asarray(MEAN), jnp.asarray(FACE), fine)

    rows_plus, rows_minus = small_call(
        join_kernel,
        [(len(PLUS_X), 2, 8, CY + CX), (len(MINUS_X), 2, 8, CY + CX)],
        [rows_plus, rows_minus, cols_plus, cols_minus],
        limit,
    )
    rows_plus = pass_on(rows_plus, "gx", 1)
    rows_minus = pass_on(rows_minus, "gx", -1)
    coarse_new = pl.pallas_call(
        base_kernel,
        out_shape=jax.ShapeDtypeStruct(coarse.shape, coarse.dtype),
        in_specs=[vmem] * 7,
        out_specs=vmem,
        scratch_shapes=[
            pltpu.VMEM((2, 2, CX + 16, CY), jnp.float32),
            pltpu.VMEM((5, CX, CY), jnp.float32),
            pltpu.VMEM((2, CX, 128), jnp.float32),
        ],
        compiler_params=limit,
        cost_estimate=pl.CostEstimate(flops=10**8, bytes_accessed=20 * 10**6, transcendentals=0),
    )(later, rows_plus, rows_minus, cols_plus, cols_minus, patchwork, covered)

    fine_new = pl.pallas_call(
        place_kernel,
        out_shape=jax.ShapeDtypeStruct((BOX_DEV,) + box, jnp.float32),
        in_specs=[hbm, hbm],
        out_specs=hbm,
        scratch_shapes=[
            pltpu.VMEM((peers, MOVE_CAP * ROWS, 128), jnp.float32),
            pltpu.SMEM((peers, 8, 128), jnp.float32),
            pltpu.SemaphoreType.DMA,
            pltpu.SemaphoreType.DMA((peers,)),
            pltpu.SemaphoreType.DMA((peers, MOVE_CAP)),
        ],
        input_output_aliases={1: 0},
        compiler_params=limit,
        cost_estimate=pl.CostEstimate(flops=0, bytes_accessed=5 * 10**6, transcendentals=0),
    )(arrived, fine_part)
    fine_new = fine_new.reshape(BOX_DEV, FIELDS, 8, BZ, 128).transpose(0, 1, 3, 2, 4)
    return coarse_new, fine_new.reshape(BOX_DEV, FIELDS, BZ, BX * BX)


def solution(mesh):
    return jax.shard_map(
        per_device,
        mesh=mesh,
        in_specs=(
            P(None, None, "gx", "gy"),
            P(("gx", "gy"), None, None, None),
            P(("gx", "gy")),
            P(None, ("gx", "gy")),
            P(("gx", "gy")),
            P(("gx", "gy")),
            P(("gx", "gy")),
        ),
        out_specs=(P(None, None, "gx", "gy"), P(("gx", "gy"), None, None, None)),
        check_vma=False,
    )
```

```python
import jax
import jax.numpy as jnp
import numpy as np
import ml_dtypes
from jax import lax
from jax.experimental import pallas as pl
from jax.experimental.pallas import tpu as pltpu
from jax.sharding import PartitionSpec as P

BX = 32
BZ = 4
HALF = 16
BOX_DEV = 32
MOVE_CAP = 2
FIELDS = 5
CHUNK = 8

COURANT = (
    (0.1, 0.2, -0.12),
    (-0.08, -0.15, 0.2),
    (0.12, 0.1, 0.18),
    (-0.05, 0.22, -0.15),
    (0.15, -0.18, -0.1),
)
CX, CY, OLD_CAP = 128, 256, 62
ROWS = FIELDS * BX


def sign(value):
    return 1 if value > 0 else -1


def first_row(sx):
    return -2 if sx > 0 else -1


def patch_maps(sx, sy):
    maps = np.zeros((128, 6, 128), np.float32)
    start = first_row(sx)

    def put(block, lane, row, col, value):
        maps[(row - start) * 20 + col, block, lane] += value

    def child(block, lane, row, col, b, e):
        put(block, lane, row, col, 1.0)
        if b:
            put(block, lane, row + 1, col, b / 8)
            put(block, lane, row - 1, col, -b / 8)
        if e:
            put(block, lane, row, col + 1, e / 8)
            put(block, lane, row, col - 1, -e / 8)

    for lane in range(128):
        xg, y = divmod(lane, 32)
        b = 1 if xg % 2 else -1
        e = 1 if y % 2 else -1
        child(0, lane, xg // 2, 2 + y // 2, b, e)
        if sx > 0 and xg == 0:
            child(1, lane, -1, 2 + y // 2, 1, e)
        if sx < 0 and xg == 3:
            child(1, lane, 2, 2 + y // 2, -1, e)
        if sy > 0 and y == 0:
            child(2, lane, xg // 2, 1, b, 1)
        if sy < 0 and y == 31:
            child(2, lane, xg // 2, 18, b, -1)
        child(3, lane, -1 if sx > 0 else 2, 2 + lane % 16, sx, 0)
        for xc in range(2):
            child(4 + xc, lane, xc, 1 if sy > 0 else 18, 0, sy)
    flat = maps.reshape(128, 768)
    return np.concatenate([flat, flat])


def mean_map():
    maps = np.zeros((128, 2, 128), np.float32)
    for source in range(128):
        xg, y = divmod(source, 32)
        for lane in range(128):
            if lane % 16 == y // 2:
                maps[source, xg // 2, lane] = 0.125
    flat = maps.reshape(128, 256)
    return np.concatenate([flat, flat])


def face_map(sx, sy):
    maps = np.zeros((128, 3, 128), np.float32)
    for source in range(128):
        xg, y = divmod(source, 32)
        for lane in range(128):
            if xg == (3 if sx > 0 else 0) and lane % 16 == y // 2:
                maps[source, 0, lane] = 0.25
            if y == (31 if sy > 0 else 0):
                maps[source, 1 + xg // 2, lane] = 0.25
    flat = maps.reshape(128, 384)
    return np.concatenate([flat, flat])


def all_maps():
    grow = np.stack([patch_maps(sign(c[1]), sign(c[2])) for c in COURANT])
    face = np.stack([face_map(sign(c[1]), sign(c[2])) for c in COURANT])
    half = ml_dtypes.bfloat16
    return grow.astype(half), mean_map().astype(half), face.astype(half)


GROW, MEAN, FACE = all_maps()


def lanes():
    return lax.broadcasted_iota(jnp.int32, (8, 128), 1)


def sublanes():
    return lax.broadcasted_iota(jnp.int32, (8, 128), 0)


def base_copies(coarse, windows, sem):
    return [
        pltpu.make_async_copy(coarse.at[:, :, :, pl.ds(64 * w, 128)], windows.at[w], sem.at[w])
        for w in (0, 2)
    ]


def cut_middle(windows):
    def rows(step, carry):
        at = pl.ds(pl.multiple_of(step * 16, 16), 16)
        lane = lax.broadcasted_iota(jnp.int32, (16, 128), 1)
        for f in range(FIELDS):
            for z in range(2):
                both = jnp.where(lane < 64, windows[2, f, z, at, :], windows[0, f, z, at, :])
                windows[1, f, z, at, :] = pltpu.roll(both, 64, 1)
        return carry

    lax.fori_loop(0, CX // 16, rows, 0)


def split_store(target, f, at, value):
    high = value.astype(jnp.bfloat16)
    target[f, at, 0:128] = high
    target[f, at, 128:256] = (value - high.astype(jnp.float32)).astype(jnp.bfloat16)


def pack(windows, packed, j, bx, by):
    which = (by >= 7).astype(jnp.int32) + (by >= 9).astype(jnp.int32)
    start = by * HALF - 2 - which * 64
    lane = lanes()
    shifts = [lax.rem(20 * i - start + 256, 128) for i in range(5)]
    for f in range(FIELDS):
        first = first_row(sign(COURANT[f][1]))
        both = []
        for z in range(2):
            held = None
            for i in range(5):
                row = windows[which, f, z, pl.ds(bx * HALF + first + i, 8, stride=2), :]
                row = pltpu.roll(row, shifts[i], 1)
                held = row if held is None else jnp.where(lane < 20 * i, held, row)
            both.append(held)
        at = pl.ds(pl.multiple_of(j * 16, 16), 16)
        split_store(packed, f, at, jnp.concatenate(both, axis=0))


def z_children(values):
    count = len(values)
    out = []
    for z in range(count):
        tilt = 0.125 * (values[(z + 1) % count] - values[(z - 1) % count])
        out += [values[z] - tilt, values[z] + tilt]
    return out


def box_rows(f, z):
    return pl.ds(32 * f + z, 8, stride=4)


def fill_fresh(box, grown, j):
    for f in range(FIELDS):
        parts = [grown[f, pl.ds(pl.multiple_of(j * 16 + 8 * z, 8), 8), 0:128] for z in range(2)]
        for z, value in enumerate(z_children(parts)):
            box[box_rows(f, z), :] = value


def upwind(values, sx, sy, sz, lane):
    out = []
    for z in range(BZ):
        v = values[z]
        vz = values[(z - sz) % BZ]
        if sx > 0:
            near = pltpu.roll(v, 32, 1)
            xs = jnp.where(lane < 32, pltpu.roll(near, 1, 0), near)
        else:
            near = pltpu.roll(v, 96, 1)
            xs = jnp.where(lane >= 96, pltpu.roll(near, 7, 0), near)
        ys = pltpu.roll(v, 1 if sy > 0 else 127, 1)
        out.append((vz, xs, ys))
    return out


def advance_field(box, out, out_at, grown, j, f):
    cz, cx, cy = COURANT[f]
    sz, sx, sy = sign(cz), sign(cx), sign(cy)
    az, ax, ay = 2 * abs(cz), 2 * abs(cx), 2 * abs(cy)
    total = az + ax + ay
    lane, sub = lanes(), sublanes()
    edge_x = ((sub == 0) & (lane < 32)) if sx > 0 else ((sub == 7) & (lane >= 96))
    edge_y = (lane % 32) == (0 if sy > 0 else 31)
    ghost_x = jnp.where(edge_x, ax, 0.0)
    gain_x = jnp.where(edge_x, 0.0, ax)
    gain_y = jnp.where(edge_y, 0.0, ay)
    rims = []
    for z in range(2):
        at = pl.ds(pl.multiple_of(j * 16 + 8 * z, 8), 8)
        rims.append(ghost_x * grown[f, at, 128:256] + ay * grown[f, at, 256:384])
    rims = z_children(rims)
    state = [box[box_rows(f, z), :] for z in range(BZ)]
    middle = []
    half_x, half_y = 0.5 * gain_x, 0.5 * gain_y
    for z, (vz, xs, ys) in enumerate(upwind(state, sx, sy, sz, lane)):
        middle.append(
            (1 - 0.5 * total) * state[z]
            + (0.5 * az) * vz
            + half_x * xs
            + half_y * ys
            + 0.5 * rims[z]
        )
    final = []
    for z, (vz, xs, ys) in enumerate(upwind(middle, sx, sy, sz, lane)):
        final.append(
            (state[z] + rims[z]) - total * middle[z] + az * vz + gain_x * xs + gain_y * ys
        )
    for z in range(BZ):
        out[pl.ds(out_at + 32 * f + z, 8, stride=4), :] = final[z]
    return middle, final


def grow(packed, maps, grown, start, stop):
    for f in range(FIELDS):
        grown[f, :, start:stop] = jnp.dot(
            packed[f], maps[f, :, start:stop], preferred_element_type=jnp.float32
        )


def int_copies(pairs, sem):
    return [
        pltpu.make_async_copy(source, target, sem.at[i]) for i, (source, target) in enumerate(pairs)
    ]


FINE_PARTS = ((0, 16), (16, 16), (32, 16), (48, OLD_CAP - 48))
GROUP = CHUNK // MOVE_CAP


def fine_copies(fine, boxes, sem):
    return [
        pltpu.make_async_copy(fine.at[pl.ds(at, n)], boxes.at[pl.ds(at, n)], sem.at[i])
        for i, (at, n) in enumerate(FINE_PARTS)
    ]


def send_kernel(
    count_in, coords_in, owner_in, slots_in, fresh_in, coarse, maps_in, fine,
    send, packed_out, sums_out, ends_out,
    count, coords, owner, slots, fresh, maps,
    windows, packed_all, sums_all, ends_all, grown, boxes, outgoing, order, ranks,
    int_sem, base_sem, map_sem, get_sem, put_sem, stash_sem,
):
    here_x, here_y = lax.axis_index("gx"), lax.axis_index("gy")
    column = lax.axis_size("gy")
    ints = int_copies(
        [
            (count_in, count), (owner_in, owner), (slots_in, slots), (coords_in, coords),
            (fresh_in, fresh),
        ],
        int_sem,
    )
    base = base_copies(coarse, windows, base_sem)
    bring_maps = pltpu.make_async_copy(maps_in, maps, map_sem)
    gets = fine_copies(fine, boxes, get_sem)
    for copy in ints + base + [bring_maps] + gets:
        copy.start()
    peers = outgoing.shape[0]
    for i in range(peers):
        ranks[i] = 0
        outgoing[i, pl.ds(MOVE_CAP * ROWS, 8), :] = jnp.full((8, 128), -1.0, jnp.float32)
    for i in range(peers * MOVE_CAP):
        order[i] = -1
    for copy in ints:
        copy.wait()

    def sort(i, c):
        dest = lax.div(owner[i], column)

        @pl.when(dest != here_x)
        def _():
            r = ranks[dest]
            order[dest * MOVE_CAP + r] = i
            ranks[dest] = r + 1
            outgoing[dest, pl.ds(MOVE_CAP * ROWS + r, 1), :] = jnp.full(
                (1, 128), slots[i].astype(jnp.float32)
            )

        return c

    lax.fori_loop(0, count[0], sort, 0)
    for copy in base:
        copy.wait()
    cut_middle(windows)
    bring_maps.wait()
    puts = []
    for group in range(peers // GROUP):
        first = group * CHUNK
        packed, sums, ends = packed_all.at[group], sums_all.at[group], ends_all.at[group]

        def lay(j, c):
            i = order[first + j]

            @pl.when(i >= 0)
            def _():
                bx = coords[0, i] - here_x * (CX // HALF)
                by = coords[1, i] - here_y * (CY // HALF)
                pack(windows, packed, j, bx, by)

            return c

        lax.fori_loop(0, CHUNK, lay, 0)
        grow(packed, maps, grown, 0, 384)
        if group == 0:
            for copy in gets:
                copy.wait()

        def step(j, c):
            i = order[first + j]

            @pl.when(i >= 0)
            def _():
                box = boxes.at[i]
                pl.when(fresh[i] > 0)(lambda: fill_fresh(box, grown, j))
                out = outgoing.at[group * GROUP + lax.div(j, MOVE_CAP)]
                out_at = lax.rem(j, MOVE_CAP) * ROWS
                for f in range(FIELDS):
                    middle, final = advance_field(box, out, out_at, grown, j, f)
                    for z in range(2):
                        at = pl.ds(pl.multiple_of(j * 16 + 8 * z, 8), 8)
                        sums[f, at, :] = final[2 * z] + final[2 * z + 1]
                        ends[f, at, :] = middle[2 * z] + middle[2 * z + 1]

            return c

        lax.fori_loop(0, CHUNK, step, 0)
        part = pl.ds(group * GROUP, GROUP)
        puts.append(pltpu.make_async_copy(outgoing.at[part], send.at[part], put_sem.at[group]))
        puts += [
            pltpu.make_async_copy(held, out.at[group], stash_sem.at[group, i])
            for i, (held, out) in enumerate(
                ((packed, packed_out), (sums, sums_out), (ends, ends_out))
            )
        ]
        for put in puts[-4:]:
            put.start()
    for put in puts:
        put.wait()


def home_kernel(
    count_in, coords_in, owner_in, slots_in, fresh_in, coarse, maps_in, mean_in, face_in, fine,
    packed_in, sums_in, ends_in,
    fine_new, patchwork, covered,
    count, coords, owner, slots, fresh, maps, mean, face, packed_all, sums_all, ends_all,
    windows, packed, grown, sums, ends, averaged, faced, boxes, kept,
    table, order, ranks, homes,
    int_sem, base_sem, map_sem, get_sem, put_sem,
):
    here_x, here_y = lax.axis_index("gx"), lax.axis_index("gy")
    column = lax.axis_size("gy")
    ints = int_copies(
        [
            (count_in, count), (owner_in, owner), (slots_in, slots), (coords_in, coords),
            (fresh_in, fresh),
        ],
        int_sem,
    )
    base = base_copies(coarse, windows, base_sem)
    bring = int_copies(
        [
            (maps_in, maps), (mean_in, mean), (face_in, face),
            (packed_in, packed_all), (sums_in, sums_all), (ends_in, ends_all),
        ],
        map_sem,
    )
    gets = fine_copies(fine, boxes, get_sem)
    for copy in ints + base + bring + gets:
        copy.start()
    for copy in ints:
        copy.wait()
    total = count[0]
    across, along = CX // HALF, CY // HALF

    def clear(i, c):
        table[i] = 0
        return c

    lax.fori_loop(0, across * along, clear, 0)

    def local(i):
        return coords[0, i] - here_x * across, coords[1, i] - here_y * along

    peers = ranks.shape[0]
    for i in range(peers):
        ranks[i] = 0
    for i in range(peers * MOVE_CAP):
        order[i] = -1

    def begin(i, n):
        bx, by = local(i)
        table[bx * along + by] = 1
        dest = lax.div(owner[i], column)
        stays = dest == here_x

        @pl.when(stays)
        def _():
            homes[n] = i

        @pl.when(jnp.logical_not(stays))
        def _():
            r = ranks[dest]
            order[dest * MOVE_CAP + r] = i
            ranks[dest] = r + 1

        return n + stays.astype(jnp.int32)

    at_home = lax.fori_loop(0, total, begin, jnp.int32(0))
    for copy in base:
        copy.wait()
    cut_middle(windows)

    def blank(step, c):
        at = pl.ds(pl.multiple_of(step * 16, 16), 16)
        for jb in range(2):
            covered[jb, at, :] = jnp.zeros((16, 128), jnp.float32)
            for f in range(FIELDS):
                for z in range(2):
                    patchwork[jb, f, z, at, :] = jnp.zeros((16, 128), jnp.float32)
        return c

    lax.fori_loop(0, CX // 16, blank, 0)

    for copy in bring + gets:
        copy.wait()

    def settle(j, i):
        bx, by = local(i)
        jb = lax.div(by, 8)
        lane = lanes()
        window = lax.div(lane, 16) == lax.rem(by, 8)
        for part in range(2):
            at = pl.ds(pl.multiple_of(bx * HALF + 8 * part, 8), 8)
            covered[jb, at, :] = jnp.where(window, 1.0, covered[jb, at, :])
        for f in range(FIELDS):
            for z in range(2):
                at = pl.ds(pl.multiple_of(j * 16 + 8 * z, 8), 8)
                for xc in range(2):
                    rows = pl.ds(bx * HALF + xc, 8, stride=2)
                    patchwork[jb, f, z, rows, :] = jnp.where(
                        window,
                        averaged[f, at, 128 * xc : 128 * xc + 128],
                        patchwork[jb, f, z, rows, :],
                    )

        def x_side(high):
            row = bx * HALF + (HALF if high else -1)
            for f in range(FIELDS):
                cx = COURANT[f][1]
                sx = sign(cx)
                weight = 2 * cx if high else -2 * cx
                ghost = (sx > 0) != high
                for z in range(2):
                    at = pl.ds(pl.multiple_of(j * 16 + 8 * z, 8), 8)
                    if ghost:
                        values = grown[f, at, 384:512]
                    else:
                        values = faced[f, at, 0:128]
                    line = values[7:8] if high else values[0:1]
                    old = patchwork[jb, f, z, pl.ds(row, 1), :]
                    patchwork[jb, f, z, pl.ds(row, 1), :] = old + jnp.where(
                        window[0:1], weight * line, 0.0
                    )

        def y_side(high):
            col = by * HALF + (HALF if high else -1)
            block = lax.div(col, 128)
            spot = lane == lax.rem(col, 128)
            for f in range(FIELDS):
                cy = COURANT[f][2]
                sy = sign(cy)
                weight = 2 * cy if high else -2 * cy
                ghost = (sy > 0) != high
                for z in range(2):
                    at = pl.ds(pl.multiple_of(j * 16 + 8 * z, 8), 8)
                    for xc in range(2):
                        if ghost:
                            values = grown[f, at, 512 + 128 * xc : 640 + 128 * xc]
                        else:
                            values = faced[f, at, 128 + 128 * xc : 256 + 128 * xc]
                        rows = pl.ds(bx * HALF + xc, 8, stride=2)
                        old = patchwork[block, f, z, rows, :]
                        patchwork[block, f, z, rows, :] = old + jnp.where(
                            spot, weight * values, 0.0
                        )

        spot_at = bx * along + by
        pl.when(table[spot_at - along] == 0)(lambda: x_side(False))
        pl.when(table[spot_at + along] == 0)(lambda: x_side(True))
        pl.when(table[spot_at - 1] == 0)(lambda: y_side(False))
        pl.when(table[spot_at + 1] == 0)(lambda: y_side(True))

    def chunk(step_at, carry):
        first = step_at * CHUNK
        here = jnp.minimum(at_home - first, CHUNK)

        def lay(j, c):
            bx, by = local(homes[first + j])
            pack(windows, packed, j, bx, by)
            return c

        lax.fori_loop(0, here, lay, 0)
        grow(packed, maps, grown, 0, 768)

        def step(j, c):
            n = homes[first + j]
            box = boxes.at[n]
            pl.when(fresh[n] > 0)(lambda: fill_fresh(box, grown, j))
            out = kept.at[slots[n]]
            at = pl.ds(pl.multiple_of(j * 16, 16), 16)
            for f in range(FIELDS):
                middle, final = advance_field(box, out, 0, grown, j, f)
                split_store(
                    sums, f, at, jnp.concatenate([final[0] + final[1], final[2] + final[3]], axis=0)
                )
                split_store(
                    ends, f, at,
                    jnp.concatenate([middle[0] + middle[1], middle[2] + middle[3]], axis=0),
                )
            return c

        lax.fori_loop(0, here, step, 0)
        average()

        def place(j, c):
            settle(j, homes[first + j])
            return c

        lax.fori_loop(0, here, place, 0)
        return carry

    def average():
        for f in range(FIELDS):
            averaged[f] = jnp.dot(sums[f], mean[...], preferred_element_type=jnp.float32)
            faced[f] = jnp.dot(ends[f], face[f], preferred_element_type=jnp.float32)

    def moved(group, carry):
        grow(packed_all.at[group], maps, grown, 384, 768)
        for f in range(FIELDS):
            split_store(sums, f, slice(None), sums_all[group, f])
            split_store(ends, f, slice(None), ends_all[group, f])
        average()

        def place(j, c):
            i = order[group * CHUNK + j]
            pl.when(i >= 0)(lambda: settle(j, i))
            return c

        lax.fori_loop(0, CHUNK, place, 0)
        return carry

    lax.fori_loop(0, lax.div(at_home + CHUNK - 1, CHUNK), chunk, 0)
    put = pltpu.make_async_copy(kept, fine_new, put_sem)
    put.start()
    lax.fori_loop(0, peers // GROUP, moved, 0)
    put.wait()


def place_kernel(arrived, fine_part, fine_new, told, tell_sem, put_sem):
    del fine_part
    tell = pltpu.make_async_copy(arrived.at[:, pl.ds(MOVE_CAP * ROWS, 8), :], told, tell_sem)
    tell.start()
    peers = arrived.shape[0]

    def put(s, r):
        slot = told[s, r, 0].astype(jnp.int32)
        copy = pltpu.make_async_copy(
            arrived.at[s, pl.ds(r * ROWS, ROWS), :],
            fine_new.at[jnp.maximum(slot, 0)],
            put_sem.at[s, r],
        )
        return slot >= 0, copy

    tell.wait()
    for action in ("start", "wait"):
        for s in range(peers):
            for r in range(MOVE_CAP):
                valid, copy = put(s, r)
                pl.when(valid)(getattr(copy, action))


PLUS_X = [f for f in range(FIELDS) if COURANT[f][1] > 0]
MINUS_X = [f for f in range(FIELDS) if COURANT[f][1] < 0]
PLUS_Y = [f for f in range(FIELDS) if COURANT[f][2] > 0]
MINUS_Y = [f for f in range(FIELDS) if COURANT[f][2] < 0]


def edge_kernel(coarse, rows_plus, rows_minus, cols_plus, cols_minus):
    for at, f in enumerate(PLUS_X):
        rows_plus[at] = coarse[f, :, CX - 8 :, :]
    for at, f in enumerate(MINUS_X):
        rows_minus[at] = coarse[f, :, 0:8, :]
    for z in range(2):
        for at, f in enumerate(PLUS_Y):
            cols_plus[at, z] = jnp.transpose(coarse[f, z, :, CY - 128 :])[120:128]
        for at, f in enumerate(MINUS_Y):
            cols_minus[at, z] = jnp.transpose(coarse[f, z, :, 0:128])[0:8]


def upwind_columns(cols_plus, cols_minus, f):
    if COURANT[f][2] > 0:
        return cols_plus[PLUS_Y.index(f)]
    return cols_minus[MINUS_Y.index(f)]


def join_kernel(rows_plus, rows_minus, cols_plus, cols_minus, send_plus, send_minus):
    for fields, rows, out in (
        (PLUS_X, rows_plus, send_plus), (MINUS_X, rows_minus, send_minus),
    ):
        for at, f in enumerate(fields):
            out[at, :, :, 0:CY] = rows[at]
            out[at, :, :, CY : CY + CX] = upwind_columns(cols_plus, cols_minus, f)


def base_kernel(
    coarse, rows_plus, rows_minus, cols_plus, cols_minus, patchwork, covered, coarse_new,
    held, mids, turned,
):
    step = 32
    lane = lax.broadcasted_iota(jnp.int32, (step, CY), 1)
    full = jnp.concatenate([covered[0], covered[1]], axis=1)
    row_at = lax.broadcasted_iota(jnp.int32, (CX, CY), 0)
    lane_at = lax.broadcasted_iota(jnp.int32, (CX, CY), 1)
    below_x = jnp.where(row_at == 0, 0.0, pltpu.roll(full, 1, 0))
    above_x = jnp.where(row_at == CX - 1, 0.0, pltpu.roll(full, CX - 1, 0))
    below_y = jnp.where(lane_at == 0, 0.0, pltpu.roll(full, 1, 1))
    above_y = jnp.where(lane_at == CY - 1, 0.0, pltpu.roll(full, CY - 1, 1))
    for i, beside in enumerate((below_x, above_x, below_y, above_y)):
        mids[i] = 1.0 - beside
    mids[4] = 1.0 - full

    for f in range(FIELDS):
        cz, cx, cy = COURANT[f]
        sz, sx, sy = sign(cz), sign(cx), sign(cy)
        az, ax, ay = abs(cz), abs(cx), abs(cy)
        up_x, down_x = (0, 1) if sx > 0 else (1, 0)
        up_y, down_y = (2, 3) if sy > 0 else (3, 2)
        near_x, near_y = (7 if sx > 0 else 0), (7 if sy > 0 else 0)
        halo = rows_plus[PLUS_X.index(f)] if sx > 0 else rows_minus[MINUS_X.index(f)]
        row_slabs = [halo[z][:, 0:CY] for z in range(2)]
        columns = upwind_columns(cols_plus, cols_minus, f)
        col_slabs = [columns[z] for z in range(2)]
        corner_lane = CY + (CX - 1 if sx > 0 else 0)
        edge = 7 if sx > 0 else 8 + CX
        lane_row = lax.broadcasted_iota(jnp.int32, (8, CY), 1)
        lane_col = lax.broadcasted_iota(jnp.int32, (8, CX), 1)
        for z in range(2):
            spot = halo[z][near_y : near_y + 1, corner_lane : corner_lane + 1]
            row, col = row_slabs[z], col_slabs[z]
            far = pltpu.roll(row, 1 if sx > 0 else 7, 0)
            if sy > 0:
                along = jnp.where(lane_row == 0, spot, pltpu.roll(row, 1, 1))
            else:
                along = jnp.where(lane_row == CY - 1, spot, pltpu.roll(row, CY - 1, 1))
            mid_row = row + 0.5 * (
                az * (row_slabs[(z - sz) % 2] - row) + ax * (far - row) + ay * (along - row)
            )
            far = pltpu.roll(col, 1 if sy > 0 else 7, 0)
            if sx > 0:
                along = jnp.where(lane_col == 0, spot, pltpu.roll(col, 1, 1))
            else:
                along = jnp.where(lane_col == CX - 1, spot, pltpu.roll(col, CX - 1, 1))
            mid_col = col + 0.5 * (
                az * (col_slabs[(z - sz) % 2] - col) + ay * (far - col) + ax * (along - col)
            )
            held[0, z, 8 : 8 + CX, :] = coarse[f, z]
            held[0, z, edge : edge + 1, :] = row[near_x : near_x + 1]
            held[1, z, edge : edge + 1, :] = mid_row[near_x : near_x + 1]
            turned[z] = jnp.transpose(
                jnp.concatenate([col, mid_col, jnp.zeros((112, CX), jnp.float32)], axis=0)
            )

        def shifted(level, z, r):
            own = held[level, z, 8 + r : 8 + r + step, :]
            xs = held[level, z, 8 + r - sx : 8 + r - sx + step, :]
            col = turned[z, r : r + step, 8 * level + near_y : 8 * level + near_y + 1]
            if sy > 0:
                ys = jnp.where(lane == 0, col, pltpu.roll(own, 1, 1))
            else:
                ys = jnp.where(lane == CY - 1, col, pltpu.roll(own, CY - 1, 1))
            vz = held[level, (z - sz) % 2, 8 + r : 8 + r + step, :]
            return own, vz, xs, ys

        for z in range(2):
            for r in range(0, CX, step):
                own, vz, xs, ys = shifted(0, z, r)
                held[1, z, 8 + r : 8 + r + step, :] = own + 0.5 * (
                    az * (vz - own) + ax * (xs - own) + ay * (ys - own)
                )
        for z in range(2):
            for r in range(0, CX, step):
                own, vz, xs, ys = shifted(1, z, r)
                at = slice(r, r + step)
                value = held[0, z, 8 + r : 8 + r + step, :] + az * (vz - own)
                value += ax * (mids[up_x, at] * xs - mids[down_x, at] * own)
                value += ay * (mids[up_y, at] * ys - mids[down_y, at] * own)
                for jb in range(2):
                    cut = slice(128 * jb, 128 * jb + 128)
                    coarse_new[f, z, at, cut] = jnp.where(
                        mids[4, at, cut] > 0.5,
                        value[:, cut] + patchwork[jb, f, z, at, :],
                        patchwork[jb, f, z, at, :],
                    )


def pass_on(values, axis, step):
    count = lax.axis_size(axis)
    return lax.ppermute(values, axis, [(i, (i + step) % count) for i in range(count)])


def small_call(kernel, shapes, operands, limit):
    vmem = pl.BlockSpec(memory_space=pltpu.VMEM)
    return pl.pallas_call(
        kernel,
        out_shape=tuple(jax.ShapeDtypeStruct(shape, jnp.float32) for shape in shapes),
        in_specs=[vmem] * len(operands),
        out_specs=(vmem,) * len(shapes),
        compiler_params=limit,
        cost_estimate=pl.CostEstimate(flops=10**6, bytes_accessed=3 * 10**6, transcendentals=0),
    )(*operands)


def per_device(coarse, fine_old, old_count, box_coords, new_owner, new_slot, fresh_box):
    peers = lax.axis_size("gx")
    fine = fine_old.reshape(OLD_CAP, FIELDS, BZ, 8, 128)
    fine = fine.transpose(0, 1, 3, 2, 4).reshape(OLD_CAP, ROWS, 128)
    vmem = pl.BlockSpec(memory_space=pltpu.VMEM)
    hbm = pl.BlockSpec(memory_space=pltpu.HBM)
    box = (ROWS, 128)
    rows = CHUNK * 16
    whole = pltpu.CompilerParams(vmem_limit_bytes=60 * 1024 * 1024)
    small = pltpu.CompilerParams(vmem_limit_bytes=16 * 1024 * 1024)
    integers = (old_count, box_coords, new_owner, new_slot, fresh_box)
    held_integers = [pltpu.SMEM(values.shape, jnp.int32) for values in integers]

    send, *stash = pl.pallas_call(
        send_kernel,
        out_shape=(
            jax.ShapeDtypeStruct((peers, MOVE_CAP * ROWS + 8, 128), jnp.float32),
            jax.ShapeDtypeStruct((peers // GROUP, FIELDS, rows, 256), jnp.bfloat16),
            jax.ShapeDtypeStruct((peers // GROUP, FIELDS, rows, 128), jnp.float32),
            jax.ShapeDtypeStruct((peers // GROUP, FIELDS, rows, 128), jnp.float32),
        ),
        in_specs=[hbm] * 8,
        out_specs=(hbm,) * 4,
        scratch_shapes=held_integers
        + [
            pltpu.VMEM((FIELDS, 256, 384), jnp.bfloat16),
            pltpu.VMEM((3, FIELDS, 2, CX, 128), jnp.float32),
            pltpu.VMEM((peers // GROUP, FIELDS, rows, 256), jnp.bfloat16),
            pltpu.VMEM((peers // GROUP, FIELDS, rows, 128), jnp.float32),
            pltpu.VMEM((peers // GROUP, FIELDS, rows, 128), jnp.float32),
            pltpu.VMEM((FIELDS, rows, 384), jnp.float32),
            pltpu.VMEM((OLD_CAP,) + box, jnp.float32),
            pltpu.VMEM((peers, MOVE_CAP * ROWS + 8, 128), jnp.float32),
            pltpu.SMEM((peers * MOVE_CAP,), jnp.int32),
            pltpu.SMEM((peers,), jnp.int32),
            pltpu.SemaphoreType.DMA((5,)),
            pltpu.SemaphoreType.DMA((3,)),
            pltpu.SemaphoreType.DMA,
            pltpu.SemaphoreType.DMA((4,)),
            pltpu.SemaphoreType.DMA((peers // GROUP,)),
            pltpu.SemaphoreType.DMA((peers // GROUP, 3)),
        ],
        compiler_params=whole,
        cost_estimate=pl.CostEstimate(flops=10**8, bytes_accessed=8 * 10**6, transcendentals=0),
    )(*integers, coarse, jnp.asarray(np.ascontiguousarray(GROW[:, :, :384])), fine)
    arrived = lax.all_to_all(send, "gx", split_axis=0, concat_axis=0, tiled=True)
    later, _ = lax.optimization_barrier((coarse, send))

    rows_plus, rows_minus, cols_plus, cols_minus = small_call(
        edge_kernel,
        [
            (len(PLUS_X), 2, 8, CY), (len(MINUS_X), 2, 8, CY),
            (len(PLUS_Y), 2, 8, CX), (len(MINUS_Y), 2, 8, CX),
        ],
        [later],
        small,
    )
    cols_plus = pass_on(cols_plus, "gy", 1)
    cols_minus = pass_on(cols_minus, "gy", -1)

    rows_plus, rows_minus = small_call(
        join_kernel,
        [(len(PLUS_X), 2, 8, CY + CX), (len(MINUS_X), 2, 8, CY + CX)],
        [rows_plus, rows_minus, cols_plus, cols_minus],
        small,
    )
    rows_plus = pass_on(rows_plus, "gx", 1)
    rows_minus = pass_on(rows_minus, "gx", -1)
    fine_part, patchwork, covered = pl.pallas_call(
        home_kernel,
        out_shape=(
            jax.ShapeDtypeStruct((BOX_DEV,) + box, jnp.float32),
            jax.ShapeDtypeStruct((2, FIELDS, 2, CX, 128), jnp.float32),
            jax.ShapeDtypeStruct((2, CX, 128), jnp.float32),
        ),
        in_specs=[hbm] * 13,
        out_specs=(hbm, vmem, vmem),
        scratch_shapes=held_integers
        + [
            pltpu.VMEM((FIELDS, 256, 768), jnp.bfloat16),
            pltpu.VMEM((256, 256), jnp.bfloat16),
            pltpu.VMEM((FIELDS, 256, 384), jnp.bfloat16),
            pltpu.VMEM((peers // GROUP, FIELDS, rows, 256), jnp.bfloat16),
            pltpu.VMEM((peers // GROUP, FIELDS, rows, 128), jnp.float32),
            pltpu.VMEM((peers // GROUP, FIELDS, rows, 128), jnp.float32),
            pltpu.VMEM((3, FIELDS, 2, CX, 128), jnp.float32),
            pltpu.VMEM((FIELDS, rows, 256), jnp.bfloat16),
            pltpu.VMEM((FIELDS, rows, 768), jnp.float32),
            pltpu.VMEM((FIELDS, rows, 256), jnp.bfloat16),
            pltpu.VMEM((FIELDS, rows, 256), jnp.bfloat16),
            pltpu.VMEM((FIELDS, rows, 256), jnp.float32),
            pltpu.VMEM((FIELDS, rows, 384), jnp.float32),
            pltpu.VMEM((OLD_CAP,) + box, jnp.float32),
            pltpu.VMEM((BOX_DEV,) + box, jnp.float32),
            pltpu.SMEM(((CX // HALF) * (CY // HALF),), jnp.int32),
            pltpu.SMEM((peers * MOVE_CAP,), jnp.int32),
            pltpu.SMEM((peers,), jnp.int32),
            pltpu.SMEM((OLD_CAP,), jnp.int32),
            pltpu.SemaphoreType.DMA((5,)),
            pltpu.SemaphoreType.DMA((3,)),
            pltpu.SemaphoreType.DMA((6,)),
            pltpu.SemaphoreType.DMA((4,)),
            pltpu.SemaphoreType.DMA,
        ],
        compiler_params=whole,
        cost_estimate=pl.CostEstimate(flops=10**9, bytes_accessed=60 * 10**6, transcendentals=0),
    )(
        *integers, later, jnp.asarray(GROW), jnp.asarray(MEAN), jnp.asarray(FACE), fine,
        *stash,
    )
    coarse_new = pl.pallas_call(
        base_kernel,
        out_shape=jax.ShapeDtypeStruct(coarse.shape, coarse.dtype),
        in_specs=[vmem] * 7,
        out_specs=vmem,
        scratch_shapes=[
            pltpu.VMEM((2, 2, CX + 16, CY), jnp.float32),
            pltpu.VMEM((5, CX, CY), jnp.float32),
            pltpu.VMEM((2, CX, 128), jnp.float32),
        ],
        compiler_params=small,
        cost_estimate=pl.CostEstimate(flops=10**8, bytes_accessed=20 * 10**6, transcendentals=0),
    )(later, rows_plus, rows_minus, cols_plus, cols_minus, patchwork, covered)

    fine_new = pl.pallas_call(
        place_kernel,
        out_shape=jax.ShapeDtypeStruct((BOX_DEV,) + box, jnp.float32),
        in_specs=[vmem, hbm],
        out_specs=hbm,
        scratch_shapes=[
            pltpu.SMEM((peers, 8, 128), jnp.float32),
            pltpu.SemaphoreType.DMA,
            pltpu.SemaphoreType.DMA((peers, MOVE_CAP)),
        ],
        input_output_aliases={1: 0},
        compiler_params=small,
        cost_estimate=pl.CostEstimate(flops=0, bytes_accessed=5 * 10**6, transcendentals=0),
    )(arrived, fine_part)
    fine_new = fine_new.reshape(BOX_DEV, FIELDS, 8, BZ, 128).transpose(0, 1, 3, 2, 4)
    return coarse_new, fine_new.reshape(BOX_DEV, FIELDS, BZ, BX * BX)


def solution(mesh):
    return jax.shard_map(
        per_device,
        mesh=mesh,
        in_specs=(
            P(None, None, "gx", "gy"),
            P(("gx", "gy"), None, None, None),
            P(("gx", "gy")),
            P(None, ("gx", "gy")),
            P(("gx", "gy")),
            P(("gx", "gy")),
            P(("gx", "gy")),
        ),
        out_specs=(P(None, None, "gx", "gy"), P(("gx", "gy"), None, None, None)),
        check_vma=False,
    )
```

```python
import jax
import jax.numpy as jnp
import numpy as np
import ml_dtypes
from jax import lax
from jax.experimental import pallas as pl
from jax.experimental.pallas import tpu as pltpu
from jax.sharding import PartitionSpec as P

BX = 32
BZ = 4
HALF = 16
BOX_DEV = 32
MOVE_CAP = 2
FIELDS = 5
CHUNK = 8

COURANT = (
    (0.1, 0.2, -0.12),
    (-0.08, -0.15, 0.2),
    (0.12, 0.1, 0.18),
    (-0.05, 0.22, -0.15),
    (0.15, -0.18, -0.1),
)
CX, CY, OLD_CAP = 128, 256, 62
ROWS = FIELDS * BX


def sign(value):
    return 1 if value > 0 else -1


def first_row(sx):
    return -2 if sx > 0 else -1


def patch_maps(sx, sy):
    maps = np.zeros((128, 6, 128), np.float32)
    start = first_row(sx)

    def put(block, lane, row, col, value):
        maps[(row - start) * 20 + col, block, lane] += value

    def child(block, lane, row, col, b, e):
        put(block, lane, row, col, 1.0)
        if b:
            put(block, lane, row + 1, col, b / 8)
            put(block, lane, row - 1, col, -b / 8)
        if e:
            put(block, lane, row, col + 1, e / 8)
            put(block, lane, row, col - 1, -e / 8)

    for lane in range(128):
        xg, y = divmod(lane, 32)
        b = 1 if xg % 2 else -1
        e = 1 if y % 2 else -1
        child(0, lane, xg // 2, 2 + y // 2, b, e)
        if sx > 0 and xg == 0:
            child(1, lane, -1, 2 + y // 2, 1, e)
        if sx < 0 and xg == 3:
            child(1, lane, 2, 2 + y // 2, -1, e)
        if sy > 0 and y == 0:
            child(2, lane, xg // 2, 1, b, 1)
        if sy < 0 and y == 31:
            child(2, lane, xg // 2, 18, b, -1)
        child(3, lane, -1 if sx > 0 else 2, 2 + lane % 16, sx, 0)
        for xc in range(2):
            child(4 + xc, lane, xc, 1 if sy > 0 else 18, 0, sy)
    flat = maps.reshape(128, 768)
    return np.concatenate([flat, flat])


def mean_map():
    maps = np.zeros((128, 2, 128), np.float32)
    for source in range(128):
        xg, y = divmod(source, 32)
        for lane in range(128):
            if lane % 16 == y // 2:
                maps[source, xg // 2, lane] = 0.125
    flat = maps.reshape(128, 256)
    return np.concatenate([flat, flat])


def face_map(sx, sy):
    maps = np.zeros((128, 3, 128), np.float32)
    for source in range(128):
        xg, y = divmod(source, 32)
        for lane in range(128):
            if xg == (3 if sx > 0 else 0) and lane % 16 == y // 2:
                maps[source, 0, lane] = 0.25
            if y == (31 if sy > 0 else 0):
                maps[source, 1 + xg // 2, lane] = 0.25
    flat = maps.reshape(128, 384)
    return np.concatenate([flat, flat])


def all_maps():
    grow = np.stack([patch_maps(sign(c[1]), sign(c[2])) for c in COURANT])
    face = np.stack([face_map(sign(c[1]), sign(c[2])) for c in COURANT])
    half = ml_dtypes.bfloat16
    return grow.astype(half), mean_map().astype(half), face.astype(half)


GROW, MEAN, FACE = all_maps()


def lanes():
    return lax.broadcasted_iota(jnp.int32, (8, 128), 1)


def sublanes():
    return lax.broadcasted_iota(jnp.int32, (8, 128), 0)


def base_copies(coarse, windows, sem):
    return [
        pltpu.make_async_copy(coarse.at[:, :, :, pl.ds(64 * w, 128)], windows.at[w], sem.at[w])
        for w in (0, 2)
    ]


def cut_middle(windows):
    def rows(step, carry):
        at = pl.ds(pl.multiple_of(step * 16, 16), 16)
        lane = lax.broadcasted_iota(jnp.int32, (16, 128), 1)
        for f in range(FIELDS):
            for z in range(2):
                both = jnp.where(lane < 64, windows[2, f, z, at, :], windows[0, f, z, at, :])
                windows[1, f, z, at, :] = pltpu.roll(both, 64, 1)
        return carry

    lax.fori_loop(0, CX // 16, rows, 0)


def split_store(target, f, at, value):
    high = value.astype(jnp.bfloat16)
    target[f, at, 0:128] = high
    target[f, at, 128:256] = (value - high.astype(jnp.float32)).astype(jnp.bfloat16)


def pack(windows, packed, j, bx, by):
    which = (by >= 7).astype(jnp.int32) + (by >= 9).astype(jnp.int32)
    start = by * HALF - 2 - which * 64
    lane = lanes()
    shifts = [lax.rem(20 * i - start + 256, 128) for i in range(5)]
    for f in range(FIELDS):
        first = first_row(sign(COURANT[f][1]))
        both = []
        for z in range(2):
            held = None
            for i in range(5):
                row = windows[which, f, z, pl.ds(bx * HALF + first + i, 8, stride=2), :]
                row = pltpu.roll(row, shifts[i], 1)
                held = row if held is None else jnp.where(lane < 20 * i, held, row)
            both.append(held)
        at = pl.ds(pl.multiple_of(j * 16, 16), 16)
        split_store(packed, f, at, jnp.concatenate(both, axis=0))


def z_children(values):
    count = len(values)
    out = []
    for z in range(count):
        tilt = 0.125 * (values[(z + 1) % count] - values[(z - 1) % count])
        out += [values[z] - tilt, values[z] + tilt]
    return out


def box_rows(f, z):
    return pl.ds(32 * f + z, 8, stride=4)


def fill_fresh(box, grown, j):
    for f in range(FIELDS):
        parts = [grown[f, pl.ds(pl.multiple_of(j * 16 + 8 * z, 8), 8), 0:128] for z in range(2)]
        for z, value in enumerate(z_children(parts)):
            box[box_rows(f, z), :] = value


def upwind(values, sx, sy, sz, lane):
    out = []
    for z in range(BZ):
        v = values[z]
        vz = values[(z - sz) % BZ]
        if sx > 0:
            near = pltpu.roll(v, 32, 1)
            xs = jnp.where(lane < 32, pltpu.roll(near, 1, 0), near)
        else:
            near = pltpu.roll(v, 96, 1)
            xs = jnp.where(lane >= 96, pltpu.roll(near, 7, 0), near)
        ys = pltpu.roll(v, 1 if sy > 0 else 127, 1)
        out.append((vz, xs, ys))
    return out


def advance_field(box, out, out_at, grown, j, f):
    cz, cx, cy = COURANT[f]
    sz, sx, sy = sign(cz), sign(cx), sign(cy)
    az, ax, ay = 2 * abs(cz), 2 * abs(cx), 2 * abs(cy)
    total = az + ax + ay
    lane, sub = lanes(), sublanes()
    edge_x = ((sub == 0) & (lane < 32)) if sx > 0 else ((sub == 7) & (lane >= 96))
    edge_y = (lane % 32) == (0 if sy > 0 else 31)
    ghost_x = jnp.where(edge_x, ax, 0.0)
    gain_x = jnp.where(edge_x, 0.0, ax)
    gain_y = jnp.where(edge_y, 0.0, ay)
    rims = []
    for z in range(2):
        at = pl.ds(pl.multiple_of(j * 16 + 8 * z, 8), 8)
        rims.append(ghost_x * grown[f, at, 128:256] + ay * grown[f, at, 256:384])
    rims = z_children(rims)
    state = [box[box_rows(f, z), :] for z in range(BZ)]
    middle = []
    half_x, half_y = 0.5 * gain_x, 0.5 * gain_y
    for z, (vz, xs, ys) in enumerate(upwind(state, sx, sy, sz, lane)):
        middle.append(
            (1 - 0.5 * total) * state[z]
            + (0.5 * az) * vz
            + half_x * xs
            + half_y * ys
            + 0.5 * rims[z]
        )
    final = []
    for z, (vz, xs, ys) in enumerate(upwind(middle, sx, sy, sz, lane)):
        final.append(
            (state[z] + rims[z]) - total * middle[z] + az * vz + gain_x * xs + gain_y * ys
        )
    for z in range(BZ):
        out[pl.ds(out_at + 32 * f + z, 8, stride=4), :] = final[z]
    return middle, final


def grow(packed, maps, grown, start, stop):
    for f in range(FIELDS):
        grown[f, :, start:stop] = jnp.dot(
            packed[f], maps[f, :, start:stop], preferred_element_type=jnp.float32
        )


def int_copies(pairs, sem):
    return [
        pltpu.make_async_copy(source, target, sem.at[i]) for i, (source, target) in enumerate(pairs)
    ]


FINE_PARTS = ((0, 16), (16, 16), (32, 16), (48, OLD_CAP - 48))
GROUP = CHUNK // MOVE_CAP


def fine_copies(fine, boxes, sem):
    return [
        pltpu.make_async_copy(fine.at[pl.ds(at, n)], boxes.at[pl.ds(at, n)], sem.at[i])
        for i, (at, n) in enumerate(FINE_PARTS)
    ]


def send_kernel(
    count_in, coords_in, owner_in, slots_in, fresh_in, coarse, maps_in, fine,
    send, packed_out, sums_out, ends_out,
    count, coords, owner, slots, fresh, maps,
    windows, packed_all, sums_all, ends_all, grown, boxes, outgoing, order, ranks,
    int_sem, base_sem, map_sem, get_sem, put_sem, stash_sem,
):
    here_x, here_y = lax.axis_index("gx"), lax.axis_index("gy")
    column = lax.axis_size("gy")
    ints = int_copies(
        [
            (count_in, count), (owner_in, owner), (slots_in, slots), (coords_in, coords),
            (fresh_in, fresh),
        ],
        int_sem,
    )
    base = base_copies(coarse, windows, base_sem)
    bring_maps = pltpu.make_async_copy(maps_in, maps, map_sem)
    gets = fine_copies(fine, boxes, get_sem)
    for copy in ints + base + [bring_maps] + gets:
        copy.start()
    peers = outgoing.shape[0]
    for i in range(peers):
        ranks[i] = 0
        outgoing[i, pl.ds(MOVE_CAP * ROWS, 8), :] = jnp.full((8, 128), -1.0, jnp.float32)
    for i in range(peers * MOVE_CAP):
        order[i] = -1
    for copy in ints:
        copy.wait()

    def sort(i, c):
        dest = lax.div(owner[i], column)

        @pl.when(dest != here_x)
        def _():
            r = ranks[dest]
            order[dest * MOVE_CAP + r] = i
            ranks[dest] = r + 1
            outgoing[dest, pl.ds(MOVE_CAP * ROWS + r, 1), :] = jnp.full(
                (1, 128), slots[i].astype(jnp.float32)
            )

        return c

    lax.fori_loop(0, count[0], sort, 0)
    for copy in base:
        copy.wait()
    cut_middle(windows)
    bring_maps.wait()
    puts = []
    for group in range(peers // GROUP):
        first = group * CHUNK
        packed, sums, ends = packed_all.at[group], sums_all.at[group], ends_all.at[group]

        def lay(j, c):
            i = order[first + j]

            @pl.when(i >= 0)
            def _():
                bx = coords[0, i] - here_x * (CX // HALF)
                by = coords[1, i] - here_y * (CY // HALF)
                pack(windows, packed, j, bx, by)

            return c

        lax.fori_loop(0, CHUNK, lay, 0)
        grow(packed, maps, grown, 0, 384)
        if group == 0:
            for copy in gets:
                copy.wait()

        def step(j, c):
            i = order[first + j]

            @pl.when(i >= 0)
            def _():
                box = boxes.at[i]
                pl.when(fresh[i] > 0)(lambda: fill_fresh(box, grown, j))
                out = outgoing.at[group * GROUP + lax.div(j, MOVE_CAP)]
                out_at = lax.rem(j, MOVE_CAP) * ROWS
                for f in range(FIELDS):
                    middle, final = advance_field(box, out, out_at, grown, j, f)
                    for z in range(2):
                        at = pl.ds(pl.multiple_of(j * 16 + 8 * z, 8), 8)
                        sums[f, at, :] = final[2 * z] + final[2 * z + 1]
                        ends[f, at, :] = middle[2 * z] + middle[2 * z + 1]

            return c

        lax.fori_loop(0, CHUNK, step, 0)
        part = pl.ds(group * GROUP, GROUP)
        puts.append(pltpu.make_async_copy(outgoing.at[part], send.at[part], put_sem.at[group]))
        puts += [
            pltpu.make_async_copy(held, out.at[group], stash_sem.at[group, i])
            for i, (held, out) in enumerate(
                ((packed, packed_out), (sums, sums_out), (ends, ends_out))
            )
        ]
        for put in puts[-4:]:
            put.start()
    for put in puts:
        put.wait()


def home_kernel(
    count_in, coords_in, owner_in, slots_in, fresh_in, coarse, maps_in, mean_in, face_in, fine,
    packed_in, sums_in, ends_in, cols_plus, cols_minus,
    fine_new, coarse_new,
    count, coords, owner, slots, fresh, maps, mean, face, packed_all, sums_all, ends_all,
    windows, packed, grown, sums, ends, averaged, faced, boxes, kept, patchwork, covered,
    held, mids, turned, table, order, ranks, homes,
    int_sem, base_sem, map_sem, get_sem, put_sem,
):
    here_x, here_y = lax.axis_index("gx"), lax.axis_index("gy")
    column = lax.axis_size("gy")
    ints = int_copies(
        [
            (count_in, count), (owner_in, owner), (slots_in, slots), (coords_in, coords),
            (fresh_in, fresh),
        ],
        int_sem,
    )
    base = base_copies(coarse, windows, base_sem)
    bring = int_copies(
        [
            (maps_in, maps), (mean_in, mean), (face_in, face),
            (packed_in, packed_all), (sums_in, sums_all), (ends_in, ends_all),
        ],
        map_sem,
    )
    gets = fine_copies(fine, boxes, get_sem)
    for copy in ints + base + bring + gets:
        copy.start()
    for copy in ints:
        copy.wait()
    total = count[0]
    across, along = CX // HALF, CY // HALF

    def clear(i, c):
        table[i] = 0
        return c

    lax.fori_loop(0, across * along, clear, 0)

    def local(i):
        return coords[0, i] - here_x * across, coords[1, i] - here_y * along

    peers = ranks.shape[0]
    for i in range(peers):
        ranks[i] = 0
    for i in range(peers * MOVE_CAP):
        order[i] = -1

    def begin(i, n):
        bx, by = local(i)
        table[bx * along + by] = 1
        dest = lax.div(owner[i], column)
        stays = dest == here_x

        @pl.when(stays)
        def _():
            homes[n] = i

        @pl.when(jnp.logical_not(stays))
        def _():
            r = ranks[dest]
            order[dest * MOVE_CAP + r] = i
            ranks[dest] = r + 1

        return n + stays.astype(jnp.int32)

    at_home = lax.fori_loop(0, total, begin, jnp.int32(0))
    for copy in base:
        copy.wait()
    cut_middle(windows)

    def blank(step, c):
        at = pl.ds(pl.multiple_of(step * 16, 16), 16)
        for jb in range(2):
            covered[jb, at, :] = jnp.zeros((16, 128), jnp.float32)
            for f in range(FIELDS):
                for z in range(2):
                    patchwork[jb, f, z, at, :] = jnp.zeros((16, 128), jnp.float32)
        return c

    lax.fori_loop(0, CX // 16, blank, 0)

    for copy in bring + gets:
        copy.wait()

    def settle(j, i):
        bx, by = local(i)
        jb = lax.div(by, 8)
        lane = lanes()
        window = lax.div(lane, 16) == lax.rem(by, 8)
        for part in range(2):
            at = pl.ds(pl.multiple_of(bx * HALF + 8 * part, 8), 8)
            covered[jb, at, :] = jnp.where(window, 1.0, covered[jb, at, :])
        for f in range(FIELDS):
            for z in range(2):
                at = pl.ds(pl.multiple_of(j * 16 + 8 * z, 8), 8)
                for xc in range(2):
                    rows = pl.ds(bx * HALF + xc, 8, stride=2)
                    patchwork[jb, f, z, rows, :] = jnp.where(
                        window,
                        averaged[f, at, 128 * xc : 128 * xc + 128],
                        patchwork[jb, f, z, rows, :],
                    )

        def x_side(high):
            row = bx * HALF + (HALF if high else -1)
            for f in range(FIELDS):
                cx = COURANT[f][1]
                sx = sign(cx)
                weight = 2 * cx if high else -2 * cx
                ghost = (sx > 0) != high
                for z in range(2):
                    at = pl.ds(pl.multiple_of(j * 16 + 8 * z, 8), 8)
                    if ghost:
                        values = grown[f, at, 384:512]
                    else:
                        values = faced[f, at, 0:128]
                    line = values[7:8] if high else values[0:1]
                    old = patchwork[jb, f, z, pl.ds(row, 1), :]
                    patchwork[jb, f, z, pl.ds(row, 1), :] = old + jnp.where(
                        window[0:1], weight * line, 0.0
                    )

        def y_side(high):
            col = by * HALF + (HALF if high else -1)
            block = lax.div(col, 128)
            spot = lane == lax.rem(col, 128)
            for f in range(FIELDS):
                cy = COURANT[f][2]
                sy = sign(cy)
                weight = 2 * cy if high else -2 * cy
                ghost = (sy > 0) != high
                for z in range(2):
                    at = pl.ds(pl.multiple_of(j * 16 + 8 * z, 8), 8)
                    for xc in range(2):
                        if ghost:
                            values = grown[f, at, 512 + 128 * xc : 640 + 128 * xc]
                        else:
                            values = faced[f, at, 128 + 128 * xc : 256 + 128 * xc]
                        rows = pl.ds(bx * HALF + xc, 8, stride=2)
                        old = patchwork[block, f, z, rows, :]
                        patchwork[block, f, z, rows, :] = old + jnp.where(
                            spot, weight * values, 0.0
                        )

        spot_at = bx * along + by
        pl.when(table[spot_at - along] == 0)(lambda: x_side(False))
        pl.when(table[spot_at + along] == 0)(lambda: x_side(True))
        pl.when(table[spot_at - 1] == 0)(lambda: y_side(False))
        pl.when(table[spot_at + 1] == 0)(lambda: y_side(True))

    def chunk(step_at, carry):
        first = step_at * CHUNK
        here = jnp.minimum(at_home - first, CHUNK)

        def lay(j, c):
            bx, by = local(homes[first + j])
            pack(windows, packed, j, bx, by)
            return c

        lax.fori_loop(0, here, lay, 0)
        grow(packed, maps, grown, 0, 768)

        def step(j, c):
            n = homes[first + j]
            box = boxes.at[n]
            pl.when(fresh[n] > 0)(lambda: fill_fresh(box, grown, j))
            out = kept.at[slots[n]]
            at = pl.ds(pl.multiple_of(j * 16, 16), 16)
            for f in range(FIELDS):
                middle, final = advance_field(box, out, 0, grown, j, f)
                split_store(
                    sums, f, at, jnp.concatenate([final[0] + final[1], final[2] + final[3]], axis=0)
                )
                split_store(
                    ends, f, at,
                    jnp.concatenate([middle[0] + middle[1], middle[2] + middle[3]], axis=0),
                )
            return c

        lax.fori_loop(0, here, step, 0)
        average()

        def place(j, c):
            settle(j, homes[first + j])
            return c

        lax.fori_loop(0, here, place, 0)
        return carry

    def average():
        for f in range(FIELDS):
            averaged[f] = jnp.dot(sums[f], mean[...], preferred_element_type=jnp.float32)
            faced[f] = jnp.dot(ends[f], face[f], preferred_element_type=jnp.float32)

    def moved(group, carry):
        grow(packed_all.at[group], maps, grown, 384, 768)
        for f in range(FIELDS):
            split_store(sums, f, slice(None), sums_all[group, f])
            split_store(ends, f, slice(None), ends_all[group, f])
        average()

        def place(j, c):
            i = order[group * CHUNK + j]
            pl.when(i >= 0)(lambda: settle(j, i))
            return c

        lax.fori_loop(0, CHUNK, place, 0)
        return carry

    lax.fori_loop(0, lax.div(at_home + CHUNK - 1, CHUNK), chunk, 0)
    put = pltpu.make_async_copy(kept, fine_new, put_sem)
    put.start()
    lax.fori_loop(0, peers // GROUP, moved, 0)
    base_pass(windows, cols_plus, cols_minus, patchwork, covered, coarse_new, held, mids, turned)
    put.wait()


PLUS_X = [f for f in range(FIELDS) if COURANT[f][1] > 0]
MINUS_X = [f for f in range(FIELDS) if COURANT[f][1] < 0]
PLUS_Y = [f for f in range(FIELDS) if COURANT[f][2] > 0]
MINUS_Y = [f for f in range(FIELDS) if COURANT[f][2] < 0]


def edge_kernel(coarse, rows_plus, rows_minus, cols_plus, cols_minus):
    for at, f in enumerate(PLUS_X):
        rows_plus[at] = coarse[f, :, CX - 8 :, :]
    for at, f in enumerate(MINUS_X):
        rows_minus[at] = coarse[f, :, 0:8, :]
    for z in range(2):
        for at, f in enumerate(PLUS_Y):
            cols_plus[at, z] = jnp.transpose(coarse[f, z, :, CY - 128 :])[120:128]
        for at, f in enumerate(MINUS_Y):
            cols_minus[at, z] = jnp.transpose(coarse[f, z, :, 0:128])[0:8]


def upwind_columns(cols_plus, cols_minus, f):
    if COURANT[f][2] > 0:
        return cols_plus[PLUS_Y.index(f)]
    return cols_minus[MINUS_Y.index(f)]


def join_kernel(rows_plus, rows_minus, cols_plus, cols_minus, send_plus, send_minus):
    for fields, rows, out in (
        (PLUS_X, rows_plus, send_plus), (MINUS_X, rows_minus, send_minus),
    ):
        for at, f in enumerate(fields):
            out[at, :, :, 0:CY] = rows[at]
            out[at, :, :, CY : CY + CX] = upwind_columns(cols_plus, cols_minus, f)


def base_pass(
    windows, cols_plus, cols_minus, patchwork, covered, coarse_new, held, mids, turned
):
    step = 32
    lane = lax.broadcasted_iota(jnp.int32, (step, CY), 1)
    full = jnp.concatenate([covered[0], covered[1]], axis=1)
    row_at = lax.broadcasted_iota(jnp.int32, (CX, CY), 0)
    lane_at = lax.broadcasted_iota(jnp.int32, (CX, CY), 1)
    below_x = jnp.where(row_at == 0, 0.0, pltpu.roll(full, 1, 0))
    above_x = jnp.where(row_at == CX - 1, 0.0, pltpu.roll(full, CX - 1, 0))
    below_y = jnp.where(lane_at == 0, 0.0, pltpu.roll(full, 1, 1))
    above_y = jnp.where(lane_at == CY - 1, 0.0, pltpu.roll(full, CY - 1, 1))
    for i, beside in enumerate((below_x, above_x, below_y, above_y)):
        mids[i] = 1.0 - beside
    mids[4] = 1.0 - full

    for f in range(FIELDS):
        cz, cx, cy = COURANT[f]
        sz, sx, sy = sign(cz), sign(cx), sign(cy)
        az, ax, ay = abs(cz), abs(cx), abs(cy)
        up_x, down_x = (0, 1) if sx > 0 else (1, 0)
        up_y, down_y = (2, 3) if sy > 0 else (3, 2)
        near_y = 7 if sy > 0 else 0
        columns = upwind_columns(cols_plus, cols_minus, f)
        col_slabs = [columns[z] for z in range(2)]
        edge = 7 if sx > 0 else 8 + CX
        lane_col = lax.broadcasted_iota(jnp.int32, (8, CX), 1)
        for z in range(2):
            col = col_slabs[z]
            far = pltpu.roll(col, 1 if sy > 0 else 7, 0)
            if sx > 0:
                along = jnp.where(lane_col == 0, 0.0, pltpu.roll(col, 1, 1))
            else:
                along = jnp.where(lane_col == CX - 1, 0.0, pltpu.roll(col, CX - 1, 1))
            mid_col = col + 0.5 * (
                az * (col_slabs[(z - sz) % 2] - col) + ay * (far - col) + ax * (along - col)
            )
            held[0, z, 8 : 8 + CX, 0:128] = windows[0, f, z]
            held[0, z, 8 : 8 + CX, 128:256] = windows[2, f, z]
            for level in range(2):
                held[level, z, edge : edge + 1, :] = jnp.zeros((1, CY), jnp.float32)
            turned[z] = jnp.transpose(
                jnp.concatenate([col, mid_col, jnp.zeros((112, CX), jnp.float32)], axis=0)
            )

        def shifted(level, z, r):
            own = held[level, z, 8 + r : 8 + r + step, :]
            xs = held[level, z, 8 + r - sx : 8 + r - sx + step, :]
            col = turned[z, r : r + step, 8 * level + near_y : 8 * level + near_y + 1]
            if sy > 0:
                ys = jnp.where(lane == 0, col, pltpu.roll(own, 1, 1))
            else:
                ys = jnp.where(lane == CY - 1, col, pltpu.roll(own, CY - 1, 1))
            vz = held[level, (z - sz) % 2, 8 + r : 8 + r + step, :]
            return own, vz, xs, ys

        for z in range(2):
            for r in range(0, CX, step):
                own, vz, xs, ys = shifted(0, z, r)
                held[1, z, 8 + r : 8 + r + step, :] = own + 0.5 * (
                    az * (vz - own) + ax * (xs - own) + ay * (ys - own)
                )
        for z in range(2):
            for r in range(0, CX, step):
                own, vz, xs, ys = shifted(1, z, r)
                at = slice(r, r + step)
                value = held[0, z, 8 + r : 8 + r + step, :] + az * (vz - own)
                value += ax * (mids[up_x, at] * xs - mids[down_x, at] * own)
                value += ay * (mids[up_y, at] * ys - mids[down_y, at] * own)
                for jb in range(2):
                    cut = slice(128 * jb, 128 * jb + 128)
                    coarse_new[f, z, at, cut] = jnp.where(
                        mids[4, at, cut] > 0.5,
                        value[:, cut] + patchwork[jb, f, z, at, :],
                        patchwork[jb, f, z, at, :],
                    )


def finish_kernel(
    arrived, rows_plus, rows_minus, fine_part, coarse_part, fine_new, coarse_new,
    held, slab, told, tell_sem, get_sem, put_sem, slab_sem,
):
    del fine_part, coarse_part
    tell = pltpu.make_async_copy(arrived.at[:, pl.ds(MOVE_CAP * ROWS, 8), :], told, tell_sem)
    tell.start()
    peers = arrived.shape[0]
    gets = [
        pltpu.make_async_copy(
            arrived.at[s, pl.ds(0, MOVE_CAP * ROWS), :], held.at[s], get_sem.at[s]
        )
        for s in range(peers)
    ]

    def spot_of(f):
        first = 0 if COURANT[f][1] > 0 else CX - 8
        return coarse_new.at[f, :, pl.ds(first, 8), :]

    slab_gets = [
        pltpu.make_async_copy(spot_of(f), slab.at[f], slab_sem.at[0, f]) for f in range(FIELDS)
    ]
    slab_puts = [
        pltpu.make_async_copy(slab.at[f], spot_of(f), slab_sem.at[1, f]) for f in range(FIELDS)
    ]
    for get in gets + slab_gets:
        get.start()
    tell.wait()

    def put(s, r):
        slot = told[s, r, 0].astype(jnp.int32)
        copy = pltpu.make_async_copy(
            held.at[s, pl.ds(r * ROWS, ROWS), :],
            fine_new.at[jnp.maximum(slot, 0)],
            put_sem.at[s, r],
        )
        return slot >= 0, copy

    for s in range(peers):
        gets[s].wait()
        for r in range(MOVE_CAP):
            valid, copy = put(s, r)
            pl.when(valid)(copy.start)

    lane = lax.broadcasted_iota(jnp.int32, (8, CY), 1)
    sub = lax.broadcasted_iota(jnp.int32, (8, CY), 0)
    for f in range(FIELDS):
        cz, cx, cy = COURANT[f]
        sz, sx, sy = sign(cz), sign(cx), sign(cy)
        az, ax, ay = abs(cz), abs(cx), abs(cy)
        near_y = 7 if sy > 0 else 0
        halo = rows_plus[PLUS_X.index(f)] if sx > 0 else rows_minus[MINUS_X.index(f)]
        rows = [halo[z][:, 0:CY] for z in range(2)]
        corner_lane = CY + (CX - 1 if sx > 0 else 0)
        slab_gets[f].wait()
        for z in range(2):
            row, row_z = rows[z], rows[(z - sz) % 2]
            corner = halo[z][near_y : near_y + 1, corner_lane : corner_lane + 1]
            far = pltpu.roll(row, 1 if sx > 0 else 7, 0)
            if sy > 0:
                along = jnp.where(lane == 0, corner, pltpu.roll(row, 1, 1))
            else:
                along = jnp.where(lane == CY - 1, corner, pltpu.roll(row, CY - 1, 1))
            middle = row + 0.5 * (az * (row_z - row) + ax * (far - row) + ay * (along - row))
            first = ax * middle + (0.5 * ax) * (
                az * row_z + ay * along - (az + ax + ay) * row
            )
            second = (0.5 * ax * ax) * row
            if sx > 0:
                first, second, at = pltpu.roll(first, 1, 0), pltpu.roll(second, 2, 0), (0, 1)
            else:
                first, second, at = pltpu.roll(first, 7, 0), pltpu.roll(second, 6, 0), (7, 6)
            slab[f, z] = (
                slab[f, z]
                + jnp.where(sub == at[0], first, 0.0)
                + jnp.where(sub == at[1], second, 0.0)
            )
        slab_puts[f].start()
    for s in range(peers):
        for r in range(MOVE_CAP):
            valid, copy = put(s, r)
            pl.when(valid)(copy.wait)
    for copy in slab_puts:
        copy.wait()


def pass_on(values, axis, step):
    count = lax.axis_size(axis)
    return lax.ppermute(values, axis, [(i, (i + step) % count) for i in range(count)])


def small_call(kernel, shapes, operands, limit):
    vmem = pl.BlockSpec(memory_space=pltpu.VMEM)
    return pl.pallas_call(
        kernel,
        out_shape=tuple(jax.ShapeDtypeStruct(shape, jnp.float32) for shape in shapes),
        in_specs=[vmem] * len(operands),
        out_specs=(vmem,) * len(shapes),
        compiler_params=limit,
        cost_estimate=pl.CostEstimate(flops=10**6, bytes_accessed=3 * 10**6, transcendentals=0),
    )(*operands)


def per_device(coarse, fine_old, old_count, box_coords, new_owner, new_slot, fresh_box):
    peers = lax.axis_size("gx")
    fine = fine_old.reshape(OLD_CAP, FIELDS, BZ, 8, 128)
    fine = fine.transpose(0, 1, 3, 2, 4).reshape(OLD_CAP, ROWS, 128)
    vmem = pl.BlockSpec(memory_space=pltpu.VMEM)
    hbm = pl.BlockSpec(memory_space=pltpu.HBM)
    box = (ROWS, 128)
    rows = CHUNK * 16
    whole = pltpu.CompilerParams(vmem_limit_bytes=60 * 1024 * 1024)
    small = pltpu.CompilerParams(vmem_limit_bytes=16 * 1024 * 1024)
    integers = (old_count, box_coords, new_owner, new_slot, fresh_box)
    held_integers = [pltpu.SMEM(values.shape, jnp.int32) for values in integers]

    send, *stash = pl.pallas_call(
        send_kernel,
        out_shape=(
            jax.ShapeDtypeStruct((peers, MOVE_CAP * ROWS + 8, 128), jnp.float32),
            jax.ShapeDtypeStruct((peers // GROUP, FIELDS, rows, 256), jnp.bfloat16),
            jax.ShapeDtypeStruct((peers // GROUP, FIELDS, rows, 128), jnp.float32),
            jax.ShapeDtypeStruct((peers // GROUP, FIELDS, rows, 128), jnp.float32),
        ),
        in_specs=[hbm] * 8,
        out_specs=(hbm,) * 4,
        scratch_shapes=held_integers
        + [
            pltpu.VMEM((FIELDS, 256, 384), jnp.bfloat16),
            pltpu.VMEM((3, FIELDS, 2, CX, 128), jnp.float32),
            pltpu.VMEM((peers // GROUP, FIELDS, rows, 256), jnp.bfloat16),
            pltpu.VMEM((peers // GROUP, FIELDS, rows, 128), jnp.float32),
            pltpu.VMEM((peers // GROUP, FIELDS, rows, 128), jnp.float32),
            pltpu.VMEM((FIELDS, rows, 384), jnp.float32),
            pltpu.VMEM((OLD_CAP,) + box, jnp.float32),
            pltpu.VMEM((peers, MOVE_CAP * ROWS + 8, 128), jnp.float32),
            pltpu.SMEM((peers * MOVE_CAP,), jnp.int32),
            pltpu.SMEM((peers,), jnp.int32),
            pltpu.SemaphoreType.DMA((5,)),
            pltpu.SemaphoreType.DMA((3,)),
            pltpu.SemaphoreType.DMA,
            pltpu.SemaphoreType.DMA((4,)),
            pltpu.SemaphoreType.DMA((peers // GROUP,)),
            pltpu.SemaphoreType.DMA((peers // GROUP, 3)),
        ],
        compiler_params=whole,
        cost_estimate=pl.CostEstimate(flops=10**8, bytes_accessed=8 * 10**6, transcendentals=0),
    )(*integers, coarse, jnp.asarray(np.ascontiguousarray(GROW[:, :, :384])), fine)
    arrived = lax.all_to_all(send, "gx", split_axis=0, concat_axis=0, tiled=True)
    later, _ = lax.optimization_barrier((coarse, send))

    rows_plus, rows_minus, cols_plus, cols_minus = small_call(
        edge_kernel,
        [
            (len(PLUS_X), 2, 8, CY), (len(MINUS_X), 2, 8, CY),
            (len(PLUS_Y), 2, 8, CX), (len(MINUS_Y), 2, 8, CX),
        ],
        [later],
        small,
    )
    cols_plus = pass_on(cols_plus, "gy", 1)
    cols_minus = pass_on(cols_minus, "gy", -1)

    rows_plus, rows_minus = small_call(
        join_kernel,
        [(len(PLUS_X), 2, 8, CY + CX), (len(MINUS_X), 2, 8, CY + CX)],
        [rows_plus, rows_minus, cols_plus, cols_minus],
        small,
    )
    rows_plus = pass_on(rows_plus, "gx", 1)
    rows_minus = pass_on(rows_minus, "gx", -1)
    fine_part, coarse_part = pl.pallas_call(
        home_kernel,
        out_shape=(
            jax.ShapeDtypeStruct((BOX_DEV,) + box, jnp.float32),
            jax.ShapeDtypeStruct(coarse.shape, jnp.float32),
        ),
        in_specs=[hbm] * 13 + [vmem] * 2,
        out_specs=(hbm, vmem),
        scratch_shapes=held_integers
        + [
            pltpu.VMEM((FIELDS, 256, 768), jnp.bfloat16),
            pltpu.VMEM((256, 256), jnp.bfloat16),
            pltpu.VMEM((FIELDS, 256, 384), jnp.bfloat16),
            pltpu.VMEM((peers // GROUP, FIELDS, rows, 256), jnp.bfloat16),
            pltpu.VMEM((peers // GROUP, FIELDS, rows, 128), jnp.float32),
            pltpu.VMEM((peers // GROUP, FIELDS, rows, 128), jnp.float32),
            pltpu.VMEM((3, FIELDS, 2, CX, 128), jnp.float32),
            pltpu.VMEM((FIELDS, rows, 256), jnp.bfloat16),
            pltpu.VMEM((FIELDS, rows, 768), jnp.float32),
            pltpu.VMEM((FIELDS, rows, 256), jnp.bfloat16),
            pltpu.VMEM((FIELDS, rows, 256), jnp.bfloat16),
            pltpu.VMEM((FIELDS, rows, 256), jnp.float32),
            pltpu.VMEM((FIELDS, rows, 384), jnp.float32),
            pltpu.VMEM((OLD_CAP,) + box, jnp.float32),
            pltpu.VMEM((BOX_DEV,) + box, jnp.float32),
            pltpu.VMEM((2, FIELDS, 2, CX, 128), jnp.float32),
            pltpu.VMEM((2, CX, 128), jnp.float32),
            pltpu.VMEM((2, 2, CX + 16, CY), jnp.float32),
            pltpu.VMEM((5, CX, CY), jnp.float32),
            pltpu.VMEM((2, CX, 128), jnp.float32),
            pltpu.SMEM(((CX // HALF) * (CY // HALF),), jnp.int32),
            pltpu.SMEM((peers * MOVE_CAP,), jnp.int32),
            pltpu.SMEM((peers,), jnp.int32),
            pltpu.SMEM((OLD_CAP,), jnp.int32),
            pltpu.SemaphoreType.DMA((5,)),
            pltpu.SemaphoreType.DMA((3,)),
            pltpu.SemaphoreType.DMA((6,)),
            pltpu.SemaphoreType.DMA((4,)),
            pltpu.SemaphoreType.DMA,
        ],
        compiler_params=whole,
        cost_estimate=pl.CostEstimate(flops=10**9, bytes_accessed=60 * 10**6, transcendentals=0),
    )(
        *integers, later, jnp.asarray(GROW), jnp.asarray(MEAN), jnp.asarray(FACE), fine,
        *stash, cols_plus, cols_minus,
    )
    fine_new, coarse_new = pl.pallas_call(
        finish_kernel,
        out_shape=(
            jax.ShapeDtypeStruct((BOX_DEV,) + box, jnp.float32),
            jax.ShapeDtypeStruct(coarse.shape, coarse.dtype),
        ),
        in_specs=[hbm, vmem, vmem, hbm, hbm],
        out_specs=(hbm, hbm),
        scratch_shapes=[
            pltpu.VMEM((peers, MOVE_CAP * ROWS, 128), jnp.float32),
            pltpu.VMEM((FIELDS, 2, 8, CY), jnp.float32),
            pltpu.SMEM((peers, 8, 128), jnp.float32),
            pltpu.SemaphoreType.DMA,
            pltpu.SemaphoreType.DMA((peers,)),
            pltpu.SemaphoreType.DMA((peers, MOVE_CAP)),
            pltpu.SemaphoreType.DMA((2, FIELDS)),
        ],
        input_output_aliases={3: 0, 4: 1},
        compiler_params=small,
        cost_estimate=pl.CostEstimate(flops=0, bytes_accessed=5 * 10**6, transcendentals=0),
    )(arrived, rows_plus, rows_minus, fine_part, coarse_part)
    fine_new = fine_new.reshape(BOX_DEV, FIELDS, 8, BZ, 128).transpose(0, 1, 3, 2, 4)
    return coarse_new, fine_new.reshape(BOX_DEV, FIELDS, BZ, BX * BX)


def solution(mesh):
    return jax.shard_map(
        per_device,
        mesh=mesh,
        in_specs=(
            P(None, None, "gx", "gy"),
            P(("gx", "gy"), None, None, None),
            P(("gx", "gy")),
            P(None, ("gx", "gy")),
            P(("gx", "gy")),
            P(("gx", "gy")),
            P(("gx", "gy")),
        ),
        out_specs=(P(None, None, "gx", "gy"), P(("gx", "gy"), None, None, None)),
        check_vma=False,
    )
```

```python
import jax
import jax.numpy as jnp
import numpy as np
import ml_dtypes
from jax import lax
from jax.experimental import pallas as pl
from jax.experimental.pallas import tpu as pltpu
from jax.sharding import PartitionSpec as P

BX = 32
BZ = 4
HALF = 16
BOX_DEV = 32
MOVE_CAP = 2
FIELDS = 5
CHUNK = 8

COURANT = (
    (0.1, 0.2, -0.12),
    (-0.08, -0.15, 0.2),
    (0.12, 0.1, 0.18),
    (-0.05, 0.22, -0.15),
    (0.15, -0.18, -0.1),
)
CX, CY, OLD_CAP = 128, 256, 62
ROWS = FIELDS * BX


def sign(value):
    return 1 if value > 0 else -1


def first_row(sx):
    return -2 if sx > 0 else -1


def patch_maps(sx, sy):
    maps = np.zeros((128, 6, 128), np.float32)
    start = first_row(sx)

    def put(block, lane, row, col, value):
        maps[(row - start) * 20 + col, block, lane] += value

    def child(block, lane, row, col, b, e):
        put(block, lane, row, col, 1.0)
        if b:
            put(block, lane, row + 1, col, b / 8)
            put(block, lane, row - 1, col, -b / 8)
        if e:
            put(block, lane, row, col + 1, e / 8)
            put(block, lane, row, col - 1, -e / 8)

    for lane in range(128):
        xg, y = divmod(lane, 32)
        b = 1 if xg % 2 else -1
        e = 1 if y % 2 else -1
        child(0, lane, xg // 2, 2 + y // 2, b, e)
        if sx > 0 and xg == 0:
            child(1, lane, -1, 2 + y // 2, 1, e)
        if sx < 0 and xg == 3:
            child(1, lane, 2, 2 + y // 2, -1, e)
        if sy > 0 and y == 0:
            child(2, lane, xg // 2, 1, b, 1)
        if sy < 0 and y == 31:
            child(2, lane, xg // 2, 18, b, -1)
        child(3, lane, -1 if sx > 0 else 2, 2 + lane % 16, sx, 0)
        for xc in range(2):
            child(4 + xc, lane, xc, 1 if sy > 0 else 18, 0, sy)
    flat = maps.reshape(128, 768)
    return np.concatenate([flat, flat])


def mean_map():
    maps = np.zeros((128, 2, 128), np.float32)
    for source in range(128):
        xg, y = divmod(source, 32)
        for lane in range(128):
            if lane % 16 == y // 2:
                maps[source, xg // 2, lane] = 0.125
    flat = maps.reshape(128, 256)
    return np.concatenate([flat, flat])


def face_map(sx, sy):
    maps = np.zeros((128, 3, 128), np.float32)
    for source in range(128):
        xg, y = divmod(source, 32)
        for lane in range(128):
            if xg == (3 if sx > 0 else 0) and lane % 16 == y // 2:
                maps[source, 0, lane] = 0.25
            if y == (31 if sy > 0 else 0):
                maps[source, 1 + xg // 2, lane] = 0.25
    flat = maps.reshape(128, 384)
    return np.concatenate([flat, flat])


def all_maps():
    grow = np.stack([patch_maps(sign(c[1]), sign(c[2])) for c in COURANT])
    face = np.stack([face_map(sign(c[1]), sign(c[2])) for c in COURANT])
    half = ml_dtypes.bfloat16
    return grow.astype(half), mean_map().astype(half), face.astype(half)


GROW, MEAN, FACE = all_maps()


def lanes():
    return lax.broadcasted_iota(jnp.int32, (8, 128), 1)


def sublanes():
    return lax.broadcasted_iota(jnp.int32, (8, 128), 0)


def base_copies(coarse, windows, sem):
    return [
        pltpu.make_async_copy(coarse.at[:, :, :, pl.ds(64 * w, 128)], windows.at[w], sem.at[w])
        for w in (0, 2)
    ]


def cut_middle(windows):
    def rows(step, carry):
        at = pl.ds(pl.multiple_of(step * 16, 16), 16)
        lane = lax.broadcasted_iota(jnp.int32, (16, 128), 1)
        for f in range(FIELDS):
            for z in range(2):
                both = jnp.where(lane < 64, windows[2, f, z, at, :], windows[0, f, z, at, :])
                windows[1, f, z, at, :] = pltpu.roll(both, 64, 1)
        return carry

    lax.fori_loop(0, CX // 16, rows, 0)


def split_store(target, f, at, value):
    high = value.astype(jnp.bfloat16)
    target[f, at, 0:128] = high
    target[f, at, 128:256] = (value - high.astype(jnp.float32)).astype(jnp.bfloat16)


def pack(windows, packed, j, bx, by):
    which = (by >= 7).astype(jnp.int32) + (by >= 9).astype(jnp.int32)
    start = by * HALF - 2 - which * 64
    lane = lanes()
    shifts = [lax.rem(20 * i - start + 256, 128) for i in range(5)]
    for f in range(FIELDS):
        first = first_row(sign(COURANT[f][1]))
        both = []
        for z in range(2):
            held = None
            for i in range(5):
                row = windows[which, f, z, pl.ds(bx * HALF + first + i, 8, stride=2), :]
                row = pltpu.roll(row, shifts[i], 1)
                held = row if held is None else jnp.where(lane < 20 * i, held, row)
            both.append(held)
        at = pl.ds(pl.multiple_of(j * 16, 16), 16)
        split_store(packed, f, at, jnp.concatenate(both, axis=0))


def z_children(values):
    count = len(values)
    out = []
    for z in range(count):
        tilt = 0.125 * (values[(z + 1) % count] - values[(z - 1) % count])
        out += [values[z] - tilt, values[z] + tilt]
    return out


def box_rows(f, z):
    return pl.ds(32 * f + z, 8, stride=4)


def fill_fresh(box, grown, j):
    for f in range(FIELDS):
        parts = [grown[f, pl.ds(pl.multiple_of(j * 16 + 8 * z, 8), 8), 0:128] for z in range(2)]
        for z, value in enumerate(z_children(parts)):
            box[box_rows(f, z), :] = value


def upwind(values, sx, sy, sz, lane):
    out = []
    for z in range(BZ):
        v = values[z]
        vz = values[(z - sz) % BZ]
        if sx > 0:
            near = pltpu.roll(v, 32, 1)
            xs = jnp.where(lane < 32, pltpu.roll(near, 1, 0), near)
        else:
            near = pltpu.roll(v, 96, 1)
            xs = jnp.where(lane >= 96, pltpu.roll(near, 7, 0), near)
        ys = pltpu.roll(v, 1 if sy > 0 else 127, 1)
        out.append((vz, xs, ys))
    return out


def advance_field(box, out, out_at, grown, j, f):
    cz, cx, cy = COURANT[f]
    sz, sx, sy = sign(cz), sign(cx), sign(cy)
    az, ax, ay = 2 * abs(cz), 2 * abs(cx), 2 * abs(cy)
    total = az + ax + ay
    lane, sub = lanes(), sublanes()
    edge_x = ((sub == 0) & (lane < 32)) if sx > 0 else ((sub == 7) & (lane >= 96))
    edge_y = (lane % 32) == (0 if sy > 0 else 31)
    ghost_x = jnp.where(edge_x, ax, 0.0)
    gain_x = jnp.where(edge_x, 0.0, ax)
    gain_y = jnp.where(edge_y, 0.0, ay)
    rims = []
    for z in range(2):
        at = pl.ds(pl.multiple_of(j * 16 + 8 * z, 8), 8)
        rims.append(ghost_x * grown[f, at, 128:256] + ay * grown[f, at, 256:384])
    rims = z_children(rims)
    state = [box[box_rows(f, z), :] for z in range(BZ)]
    middle = []
    half_x, half_y = 0.5 * gain_x, 0.5 * gain_y
    for z, (vz, xs, ys) in enumerate(upwind(state, sx, sy, sz, lane)):
        middle.append(
            (1 - 0.5 * total) * state[z]
            + (0.5 * az) * vz
            + half_x * xs
            + half_y * ys
            + 0.5 * rims[z]
        )
    final = []
    for z, (vz, xs, ys) in enumerate(upwind(middle, sx, sy, sz, lane)):
        final.append(
            (state[z] + rims[z]) - total * middle[z] + az * vz + gain_x * xs + gain_y * ys
        )
    for z in range(BZ):
        out[pl.ds(out_at + 32 * f + z, 8, stride=4), :] = final[z]
    return middle, final


def grow(packed, maps, grown, start, stop):
    for f in range(FIELDS):
        grown[f, :, start:stop] = jnp.dot(
            packed[f], maps[f, :, start:stop], preferred_element_type=jnp.float32
        )


def int_copies(pairs, sem):
    return [
        pltpu.make_async_copy(source, target, sem.at[i]) for i, (source, target) in enumerate(pairs)
    ]


def in_pairs(body):
    def two(pair, c):
        body(2 * pair)
        body(2 * pair + 1)
        return c

    lax.fori_loop(0, CHUNK // 2, two, 0)


FINE_PARTS = ((0, 16), (16, 16), (32, 16), (48, OLD_CAP - 48))
GROUP = CHUNK // MOVE_CAP


def fine_copies(fine, boxes, sem):
    return [
        pltpu.make_async_copy(fine.at[pl.ds(at, n)], boxes.at[pl.ds(at, n)], sem.at[i])
        for i, (at, n) in enumerate(FINE_PARTS)
    ]


def send_kernel(
    count_in, coords_in, owner_in, slots_in, fresh_in, coarse, maps_in, fine,
    send, packed_out, sums_out, ends_out,
    count, coords, owner, slots, fresh, maps,
    windows, packed_all, sums_all, ends_all, grown, boxes, outgoing, order, ranks,
    int_sem, base_sem, map_sem, get_sem, put_sem, stash_sem,
):
    here_x, here_y = lax.axis_index("gx"), lax.axis_index("gy")
    column = lax.axis_size("gy")
    ints = int_copies(
        [
            (count_in, count), (owner_in, owner), (slots_in, slots), (coords_in, coords),
            (fresh_in, fresh),
        ],
        int_sem,
    )
    base = base_copies(coarse, windows, base_sem)
    bring_maps = pltpu.make_async_copy(maps_in, maps, map_sem)
    gets = fine_copies(fine, boxes, get_sem)
    for copy in ints + base + [bring_maps] + gets:
        copy.start()
    peers = outgoing.shape[0]
    for i in range(peers):
        ranks[i] = 0
        outgoing[i, pl.ds(MOVE_CAP * ROWS, 8), :] = jnp.full((8, 128), -1.0, jnp.float32)
    for i in range(peers * MOVE_CAP):
        order[i] = -1
    for copy in ints:
        copy.wait()

    def sort(i, c):
        dest = lax.div(owner[i], column)

        @pl.when(dest != here_x)
        def _():
            r = ranks[dest]
            order[dest * MOVE_CAP + r] = i
            ranks[dest] = r + 1
            outgoing[dest, pl.ds(MOVE_CAP * ROWS + r, 1), :] = jnp.full(
                (1, 128), slots[i].astype(jnp.float32)
            )

        return c

    lax.fori_loop(0, count[0], sort, 0)
    for copy in base:
        copy.wait()
    cut_middle(windows)
    bring_maps.wait()
    puts = []
    for group in range(peers // GROUP):
        first = group * CHUNK
        packed, sums, ends = packed_all.at[group], sums_all.at[group], ends_all.at[group]

        def lay(j):
            i = jnp.maximum(order[first + j], 0)
            bx = jnp.clip(coords[0, i] - here_x * (CX // HALF), 1, CX // HALF - 2)
            by = jnp.clip(coords[1, i] - here_y * (CY // HALF), 1, CY // HALF - 2)
            pack(windows, packed, j, bx, by)

        in_pairs(lay)
        grow(packed, maps, grown, 0, 384)
        if group == 0:
            for copy in gets:
                copy.wait()

        def renew(j, c):
            i = order[first + j]
            valid = (i >= 0) & (fresh[jnp.maximum(i, 0)] > 0)
            pl.when(valid)(lambda: fill_fresh(boxes.at[i], grown, j))
            return c

        lax.fori_loop(0, CHUNK, renew, 0)

        def step(j):
            box = boxes.at[jnp.maximum(order[first + j], 0)]
            out = outgoing.at[group * GROUP + lax.div(j, MOVE_CAP)]
            out_at = lax.rem(j, MOVE_CAP) * ROWS
            for f in range(FIELDS):
                middle, final = advance_field(box, out, out_at, grown, j, f)
                for z in range(2):
                    at = pl.ds(pl.multiple_of(j * 16 + 8 * z, 8), 8)
                    sums[f, at, :] = final[2 * z] + final[2 * z + 1]
                    ends[f, at, :] = middle[2 * z] + middle[2 * z + 1]

        in_pairs(step)
        part = pl.ds(group * GROUP, GROUP)
        puts.append(pltpu.make_async_copy(outgoing.at[part], send.at[part], put_sem.at[group]))
        puts += [
            pltpu.make_async_copy(held, out.at[group], stash_sem.at[group, i])
            for i, (held, out) in enumerate(
                ((packed, packed_out), (sums, sums_out), (ends, ends_out))
            )
        ]
        for put in puts[-4:]:
            put.start()
    for put in puts:
        put.wait()


def home_kernel(
    count_in, coords_in, owner_in, slots_in, fresh_in, coarse, maps_in, mean_in, face_in, fine,
    packed_in, sums_in, ends_in, cols_plus, cols_minus,
    fine_new, coarse_new,
    count, coords, owner, slots, fresh, maps, mean, face, packed_all, sums_all, ends_all,
    windows, packed, grown, sums, ends, averaged, faced, boxes, kept, patchwork, covered,
    held, mids, turned, table, order, ranks, homes,
    int_sem, base_sem, map_sem, get_sem, put_sem,
):
    here_x, here_y = lax.axis_index("gx"), lax.axis_index("gy")
    column = lax.axis_size("gy")
    ints = int_copies(
        [
            (count_in, count), (owner_in, owner), (slots_in, slots), (coords_in, coords),
            (fresh_in, fresh),
        ],
        int_sem,
    )
    base = base_copies(coarse, windows, base_sem)
    bring = int_copies(
        [
            (maps_in, maps), (mean_in, mean), (face_in, face),
            (packed_in, packed_all), (sums_in, sums_all), (ends_in, ends_all),
        ],
        map_sem,
    )
    gets = fine_copies(fine, boxes, get_sem)
    for copy in ints + base + bring + gets:
        copy.start()
    for copy in ints:
        copy.wait()
    total = count[0]
    across, along = CX // HALF, CY // HALF

    def clear(i, c):
        table[i] = 0
        return c

    lax.fori_loop(0, across * along, clear, 0)

    def local(i):
        return coords[0, i] - here_x * across, coords[1, i] - here_y * along

    peers = ranks.shape[0]
    for i in range(peers):
        ranks[i] = 0
    for i in range(peers * MOVE_CAP):
        order[i] = -1

    def begin(i, n):
        bx, by = local(i)
        table[bx * along + by] = 1
        dest = lax.div(owner[i], column)
        stays = dest == here_x

        @pl.when(stays)
        def _():
            homes[n] = i

        @pl.when(jnp.logical_not(stays))
        def _():
            r = ranks[dest]
            order[dest * MOVE_CAP + r] = i
            ranks[dest] = r + 1

        return n + stays.astype(jnp.int32)

    at_home = lax.fori_loop(0, total, begin, jnp.int32(0))
    for copy in base:
        copy.wait()
    cut_middle(windows)

    def blank(step, c):
        at = pl.ds(pl.multiple_of(step * 16, 16), 16)
        for jb in range(2):
            covered[jb, at, :] = jnp.zeros((16, 128), jnp.float32)
            for f in range(FIELDS):
                for z in range(2):
                    patchwork[jb, f, z, at, :] = jnp.zeros((16, 128), jnp.float32)
        return c

    lax.fori_loop(0, CX // 16, blank, 0)

    for copy in bring + gets:
        copy.wait()

    def settle(j, i):
        bx, by = local(i)
        jb = lax.div(by, 8)
        lane = lanes()
        window = lax.div(lane, 16) == lax.rem(by, 8)
        for part in range(2):
            at = pl.ds(pl.multiple_of(bx * HALF + 8 * part, 8), 8)
            covered[jb, at, :] = jnp.where(window, 1.0, covered[jb, at, :])
        for f in range(FIELDS):
            for z in range(2):
                at = pl.ds(pl.multiple_of(j * 16 + 8 * z, 8), 8)
                for xc in range(2):
                    rows = pl.ds(bx * HALF + xc, 8, stride=2)
                    patchwork[jb, f, z, rows, :] = jnp.where(
                        window,
                        averaged[f, at, 128 * xc : 128 * xc + 128],
                        patchwork[jb, f, z, rows, :],
                    )

        def x_side(high):
            row = bx * HALF + (HALF if high else -1)
            for f in range(FIELDS):
                cx = COURANT[f][1]
                sx = sign(cx)
                weight = 2 * cx if high else -2 * cx
                ghost = (sx > 0) != high
                for z in range(2):
                    at = pl.ds(pl.multiple_of(j * 16 + 8 * z, 8), 8)
                    if ghost:
                        values = grown[f, at, 384:512]
                    else:
                        values = faced[f, at, 0:128]
                    line = values[7:8] if high else values[0:1]
                    old = patchwork[jb, f, z, pl.ds(row, 1), :]
                    patchwork[jb, f, z, pl.ds(row, 1), :] = old + jnp.where(
                        window[0:1], weight * line, 0.0
                    )

        def y_side(high):
            col = by * HALF + (HALF if high else -1)
            block = lax.div(col, 128)
            spot = lane == lax.rem(col, 128)
            for f in range(FIELDS):
                cy = COURANT[f][2]
                sy = sign(cy)
                weight = 2 * cy if high else -2 * cy
                ghost = (sy > 0) != high
                for z in range(2):
                    at = pl.ds(pl.multiple_of(j * 16 + 8 * z, 8), 8)
                    for xc in range(2):
                        if ghost:
                            values = grown[f, at, 512 + 128 * xc : 640 + 128 * xc]
                        else:
                            values = faced[f, at, 128 + 128 * xc : 256 + 128 * xc]
                        rows = pl.ds(bx * HALF + xc, 8, stride=2)
                        old = patchwork[block, f, z, rows, :]
                        patchwork[block, f, z, rows, :] = old + jnp.where(
                            spot, weight * values, 0.0
                        )

        spot_at = bx * along + by
        pl.when(table[spot_at - along] == 0)(lambda: x_side(False))
        pl.when(table[spot_at + along] == 0)(lambda: x_side(True))
        pl.when(table[spot_at - 1] == 0)(lambda: y_side(False))
        pl.when(table[spot_at + 1] == 0)(lambda: y_side(True))

    def chunk(step_at, carry):
        first = step_at * CHUNK
        here = jnp.minimum(at_home - first, CHUNK)

        def lay(j, c):
            bx, by = local(homes[first + j])
            pack(windows, packed, j, bx, by)
            return c

        lax.fori_loop(0, here, lay, 0)
        grow(packed, maps, grown, 0, 768)

        def step(j, c):
            n = homes[first + j]
            box = boxes.at[n]
            pl.when(fresh[n] > 0)(lambda: fill_fresh(box, grown, j))
            out = kept.at[slots[n]]
            at = pl.ds(pl.multiple_of(j * 16, 16), 16)
            for f in range(FIELDS):
                middle, final = advance_field(box, out, 0, grown, j, f)
                split_store(
                    sums, f, at, jnp.concatenate([final[0] + final[1], final[2] + final[3]], axis=0)
                )
                split_store(
                    ends, f, at,
                    jnp.concatenate([middle[0] + middle[1], middle[2] + middle[3]], axis=0),
                )
            return c

        lax.fori_loop(0, here, step, 0)
        average()

        def place(j, c):
            settle(j, homes[first + j])
            return c

        lax.fori_loop(0, here, place, 0)
        return carry

    def average():
        for f in range(FIELDS):
            averaged[f] = jnp.dot(sums[f], mean[...], preferred_element_type=jnp.float32)
            faced[f] = jnp.dot(ends[f], face[f], preferred_element_type=jnp.float32)

    def moved(group, carry):
        grow(packed_all.at[group], maps, grown, 384, 768)
        for f in range(FIELDS):
            split_store(sums, f, slice(None), sums_all[group, f])
            split_store(ends, f, slice(None), ends_all[group, f])
        average()

        def place(j, c):
            i = order[group * CHUNK + j]
            pl.when(i >= 0)(lambda: settle(j, i))
            return c

        lax.fori_loop(0, CHUNK, place, 0)
        return carry

    lax.fori_loop(0, lax.div(at_home + CHUNK - 1, CHUNK), chunk, 0)
    put = pltpu.make_async_copy(kept, fine_new, put_sem)
    put.start()
    lax.fori_loop(0, peers // GROUP, moved, 0)
    base_pass(windows, cols_plus, cols_minus, patchwork, covered, coarse_new, held, mids, turned)
    put.wait()


PLUS_X = [f for f in range(FIELDS) if COURANT[f][1] > 0]
MINUS_X = [f for f in range(FIELDS) if COURANT[f][1] < 0]
PLUS_Y = [f for f in range(FIELDS) if COURANT[f][2] > 0]
MINUS_Y = [f for f in range(FIELDS) if COURANT[f][2] < 0]


def edge_kernel(coarse, rows_plus, rows_minus, cols_plus, cols_minus):
    for at, f in enumerate(PLUS_X):
        rows_plus[at] = coarse[f, :, CX - 8 :, :]
    for at, f in enumerate(MINUS_X):
        rows_minus[at] = coarse[f, :, 0:8, :]
    for z in range(2):
        for at, f in enumerate(PLUS_Y):
            cols_plus[at, z] = jnp.transpose(coarse[f, z, :, CY - 128 :])[120:128]
        for at, f in enumerate(MINUS_Y):
            cols_minus[at, z] = jnp.transpose(coarse[f, z, :, 0:128])[0:8]


def upwind_columns(cols_plus, cols_minus, f):
    if COURANT[f][2] > 0:
        return cols_plus[PLUS_Y.index(f)]
    return cols_minus[MINUS_Y.index(f)]


def join_kernel(rows_plus, rows_minus, cols_plus, cols_minus, send_plus, send_minus):
    for fields, rows, out in (
        (PLUS_X, rows_plus, send_plus), (MINUS_X, rows_minus, send_minus),
    ):
        for at, f in enumerate(fields):
            out[at, :, :, 0:CY] = rows[at]
            out[at, :, :, CY : CY + CX] = upwind_columns(cols_plus, cols_minus, f)


def base_pass(
    windows, cols_plus, cols_minus, patchwork, covered, coarse_new, held, mids, turned
):
    step = 32
    lane = lax.broadcasted_iota(jnp.int32, (step, CY), 1)
    full = jnp.concatenate([covered[0], covered[1]], axis=1)
    row_at = lax.broadcasted_iota(jnp.int32, (CX, CY), 0)
    lane_at = lax.broadcasted_iota(jnp.int32, (CX, CY), 1)
    below_x = jnp.where(row_at == 0, 0.0, pltpu.roll(full, 1, 0))
    above_x = jnp.where(row_at == CX - 1, 0.0, pltpu.roll(full, CX - 1, 0))
    below_y = jnp.where(lane_at == 0, 0.0, pltpu.roll(full, 1, 1))
    above_y = jnp.where(lane_at == CY - 1, 0.0, pltpu.roll(full, CY - 1, 1))
    for i, beside in enumerate((below_x, above_x, below_y, above_y)):
        mids[i] = 1.0 - beside
    mids[4] = 1.0 - full

    for f in range(FIELDS):
        cz, cx, cy = COURANT[f]
        sz, sx, sy = sign(cz), sign(cx), sign(cy)
        az, ax, ay = abs(cz), abs(cx), abs(cy)
        up_x, down_x = (0, 1) if sx > 0 else (1, 0)
        up_y, down_y = (2, 3) if sy > 0 else (3, 2)
        near_y = 7 if sy > 0 else 0
        columns = upwind_columns(cols_plus, cols_minus, f)
        col_slabs = [columns[z] for z in range(2)]
        edge = 7 if sx > 0 else 8 + CX
        lane_col = lax.broadcasted_iota(jnp.int32, (8, CX), 1)
        for z in range(2):
            col = col_slabs[z]
            far = pltpu.roll(col, 1 if sy > 0 else 7, 0)
            if sx > 0:
                along = jnp.where(lane_col == 0, 0.0, pltpu.roll(col, 1, 1))
            else:
                along = jnp.where(lane_col == CX - 1, 0.0, pltpu.roll(col, CX - 1, 1))
            mid_col = col + 0.5 * (
                az * (col_slabs[(z - sz) % 2] - col) + ay * (far - col) + ax * (along - col)
            )
            held[0, z, 8 : 8 + CX, 0:128] = windows[0, f, z]
            held[0, z, 8 : 8 + CX, 128:256] = windows[2, f, z]
            for level in range(2):
                held[level, z, edge : edge + 1, :] = jnp.zeros((1, CY), jnp.float32)
            turned[z] = jnp.transpose(
                jnp.concatenate([col, mid_col, jnp.zeros((112, CX), jnp.float32)], axis=0)
            )

        def shifted(level, z, r):
            own = held[level, z, 8 + r : 8 + r + step, :]
            xs = held[level, z, 8 + r - sx : 8 + r - sx + step, :]
            col = turned[z, r : r + step, 8 * level + near_y : 8 * level + near_y + 1]
            if sy > 0:
                ys = jnp.where(lane == 0, col, pltpu.roll(own, 1, 1))
            else:
                ys = jnp.where(lane == CY - 1, col, pltpu.roll(own, CY - 1, 1))
            vz = held[level, (z - sz) % 2, 8 + r : 8 + r + step, :]
            return own, vz, xs, ys

        for z in range(2):
            for r in range(0, CX, step):
                own, vz, xs, ys = shifted(0, z, r)
                held[1, z, 8 + r : 8 + r + step, :] = own + 0.5 * (
                    az * (vz - own) + ax * (xs - own) + ay * (ys - own)
                )
        for z in range(2):
            for r in range(0, CX, step):
                own, vz, xs, ys = shifted(1, z, r)
                at = slice(r, r + step)
                value = held[0, z, 8 + r : 8 + r + step, :] + az * (vz - own)
                value += ax * (mids[up_x, at] * xs - mids[down_x, at] * own)
                value += ay * (mids[up_y, at] * ys - mids[down_y, at] * own)
                for jb in range(2):
                    cut = slice(128 * jb, 128 * jb + 128)
                    coarse_new[f, z, at, cut] = jnp.where(
                        mids[4, at, cut] > 0.5,
                        value[:, cut] + patchwork[jb, f, z, at, :],
                        patchwork[jb, f, z, at, :],
                    )


def finish_kernel(
    arrived, rows_plus, rows_minus, fine_part, coarse_part, fine_new, coarse_new,
    held, slab, told, tell_sem, get_sem, put_sem, slab_sem,
):
    del fine_part, coarse_part
    tell = pltpu.make_async_copy(arrived.at[:, pl.ds(MOVE_CAP * ROWS, 8), :], told, tell_sem)
    tell.start()
    peers = arrived.shape[0]
    gets = [
        pltpu.make_async_copy(
            arrived.at[s, pl.ds(0, MOVE_CAP * ROWS), :], held.at[s], get_sem.at[s]
        )
        for s in range(peers)
    ]

    def spot_of(f):
        first = 0 if COURANT[f][1] > 0 else CX - 8
        return coarse_new.at[f, :, pl.ds(first, 8), :]

    slab_gets = [
        pltpu.make_async_copy(spot_of(f), slab.at[f], slab_sem.at[0, f]) for f in range(FIELDS)
    ]
    slab_puts = [
        pltpu.make_async_copy(slab.at[f], spot_of(f), slab_sem.at[1, f]) for f in range(FIELDS)
    ]
    for get in gets + slab_gets:
        get.start()
    tell.wait()

    def put(s, r):
        slot = told[s, r, 0].astype(jnp.int32)
        copy = pltpu.make_async_copy(
            held.at[s, pl.ds(r * ROWS, ROWS), :],
            fine_new.at[jnp.maximum(slot, 0)],
            put_sem.at[s, r],
        )
        return slot >= 0, copy

    for s in range(peers):
        gets[s].wait()
        for r in range(MOVE_CAP):
            valid, copy = put(s, r)
            pl.when(valid)(copy.start)

    lane = lax.broadcasted_iota(jnp.int32, (8, CY), 1)
    sub = lax.broadcasted_iota(jnp.int32, (8, CY), 0)
    for f in range(FIELDS):
        cz, cx, cy = COURANT[f]
        sz, sx, sy = sign(cz), sign(cx), sign(cy)
        az, ax, ay = abs(cz), abs(cx), abs(cy)
        near_y = 7 if sy > 0 else 0
        halo = rows_plus[PLUS_X.index(f)] if sx > 0 else rows_minus[MINUS_X.index(f)]
        rows = [halo[z][:, 0:CY] for z in range(2)]
        corner_lane = CY + (CX - 1 if sx > 0 else 0)
        slab_gets[f].wait()
        for z in range(2):
            row, row_z = rows[z], rows[(z - sz) % 2]
            corner = halo[z][near_y : near_y + 1, corner_lane : corner_lane + 1]
            far = pltpu.roll(row, 1 if sx > 0 else 7, 0)
            if sy > 0:
                along = jnp.where(lane == 0, corner, pltpu.roll(row, 1, 1))
            else:
                along = jnp.where(lane == CY - 1, corner, pltpu.roll(row, CY - 1, 1))
            middle = row + 0.5 * (az * (row_z - row) + ax * (far - row) + ay * (along - row))
            first = ax * middle + (0.5 * ax) * (
                az * row_z + ay * along - (az + ax + ay) * row
            )
            second = (0.5 * ax * ax) * row
            if sx > 0:
                first, second, at = pltpu.roll(first, 1, 0), pltpu.roll(second, 2, 0), (0, 1)
            else:
                first, second, at = pltpu.roll(first, 7, 0), pltpu.roll(second, 6, 0), (7, 6)
            slab[f, z] = (
                slab[f, z]
                + jnp.where(sub == at[0], first, 0.0)
                + jnp.where(sub == at[1], second, 0.0)
            )
        slab_puts[f].start()
    for s in range(peers):
        for r in range(MOVE_CAP):
            valid, copy = put(s, r)
            pl.when(valid)(copy.wait)
    for copy in slab_puts:
        copy.wait()


def pass_on(values, axis, step):
    count = lax.axis_size(axis)
    return lax.ppermute(values, axis, [(i, (i + step) % count) for i in range(count)])


def small_call(kernel, shapes, operands, limit):
    vmem = pl.BlockSpec(memory_space=pltpu.VMEM)
    return pl.pallas_call(
        kernel,
        out_shape=tuple(jax.ShapeDtypeStruct(shape, jnp.float32) for shape in shapes),
        in_specs=[vmem] * len(operands),
        out_specs=(vmem,) * len(shapes),
        compiler_params=limit,
        cost_estimate=pl.CostEstimate(flops=10**6, bytes_accessed=3 * 10**6, transcendentals=0),
    )(*operands)


def per_device(coarse, fine_old, old_count, box_coords, new_owner, new_slot, fresh_box):
    peers = lax.axis_size("gx")
    fine = fine_old.reshape(OLD_CAP, FIELDS, BZ, 8, 128)
    fine = fine.transpose(0, 1, 3, 2, 4).reshape(OLD_CAP, ROWS, 128)
    vmem = pl.BlockSpec(memory_space=pltpu.VMEM)
    hbm = pl.BlockSpec(memory_space=pltpu.HBM)
    box = (ROWS, 128)
    rows = CHUNK * 16
    whole = pltpu.CompilerParams(vmem_limit_bytes=60 * 1024 * 1024)
    small = pltpu.CompilerParams(vmem_limit_bytes=16 * 1024 * 1024)
    integers = (old_count, box_coords, new_owner, new_slot, fresh_box)
    held_integers = [pltpu.SMEM(values.shape, jnp.int32) for values in integers]

    send, *stash = pl.pallas_call(
        send_kernel,
        out_shape=(
            jax.ShapeDtypeStruct((peers, MOVE_CAP * ROWS + 8, 128), jnp.float32),
            jax.ShapeDtypeStruct((peers // GROUP, FIELDS, rows, 256), jnp.bfloat16),
            jax.ShapeDtypeStruct((peers // GROUP, FIELDS, rows, 128), jnp.float32),
            jax.ShapeDtypeStruct((peers // GROUP, FIELDS, rows, 128), jnp.float32),
        ),
        in_specs=[hbm] * 8,
        out_specs=(hbm,) * 4,
        scratch_shapes=held_integers
        + [
            pltpu.VMEM((FIELDS, 256, 384), jnp.bfloat16),
            pltpu.VMEM((3, FIELDS, 2, CX, 128), jnp.float32),
            pltpu.VMEM((peers // GROUP, FIELDS, rows, 256), jnp.bfloat16),
            pltpu.VMEM((peers // GROUP, FIELDS, rows, 128), jnp.float32),
            pltpu.VMEM((peers // GROUP, FIELDS, rows, 128), jnp.float32),
            pltpu.VMEM((FIELDS, rows, 384), jnp.float32),
            pltpu.VMEM((OLD_CAP,) + box, jnp.float32),
            pltpu.VMEM((peers, MOVE_CAP * ROWS + 8, 128), jnp.float32),
            pltpu.SMEM((peers * MOVE_CAP,), jnp.int32),
            pltpu.SMEM((peers,), jnp.int32),
            pltpu.SemaphoreType.DMA((5,)),
            pltpu.SemaphoreType.DMA((3,)),
            pltpu.SemaphoreType.DMA,
            pltpu.SemaphoreType.DMA((4,)),
            pltpu.SemaphoreType.DMA((peers // GROUP,)),
            pltpu.SemaphoreType.DMA((peers // GROUP, 3)),
        ],
        compiler_params=whole,
        cost_estimate=pl.CostEstimate(flops=10**8, bytes_accessed=8 * 10**6, transcendentals=0),
    )(*integers, coarse, jnp.asarray(np.ascontiguousarray(GROW[:, :, :384])), fine)
    arrived = lax.all_to_all(send, "gx", split_axis=0, concat_axis=0, tiled=True)
    later, _ = lax.optimization_barrier((coarse, send))

    rows_plus, rows_minus, cols_plus, cols_minus = small_call(
        edge_kernel,
        [
            (len(PLUS_X), 2, 8, CY), (len(MINUS_X), 2, 8, CY),
            (len(PLUS_Y), 2, 8, CX), (len(MINUS_Y), 2, 8, CX),
        ],
        [later],
        small,
    )
    cols_plus = pass_on(cols_plus, "gy", 1)
    cols_minus = pass_on(cols_minus, "gy", -1)

    rows_plus, rows_minus = small_call(
        join_kernel,
        [(len(PLUS_X), 2, 8, CY + CX), (len(MINUS_X), 2, 8, CY + CX)],
        [rows_plus, rows_minus, cols_plus, cols_minus],
        small,
    )
    rows_plus = pass_on(rows_plus, "gx", 1)
    rows_minus = pass_on(rows_minus, "gx", -1)
    fine_part, coarse_part = pl.pallas_call(
        home_kernel,
        out_shape=(
            jax.ShapeDtypeStruct((BOX_DEV,) + box, jnp.float32),
            jax.ShapeDtypeStruct(coarse.shape, jnp.float32),
        ),
        in_specs=[hbm] * 13 + [vmem] * 2,
        out_specs=(hbm, vmem),
        scratch_shapes=held_integers
        + [
            pltpu.VMEM((FIELDS, 256, 768), jnp.bfloat16),
            pltpu.VMEM((256, 256), jnp.bfloat16),
            pltpu.VMEM((FIELDS, 256, 384), jnp.bfloat16),
            pltpu.VMEM((peers // GROUP, FIELDS, rows, 256), jnp.bfloat16),
            pltpu.VMEM((peers // GROUP, FIELDS, rows, 128), jnp.float32),
            pltpu.VMEM((peers // GROUP, FIELDS, rows, 128), jnp.float32),
            pltpu.VMEM((3, FIELDS, 2, CX, 128), jnp.float32),
            pltpu.VMEM((FIELDS, rows, 256), jnp.bfloat16),
            pltpu.VMEM((FIELDS, rows, 768), jnp.float32),
            pltpu.VMEM((FIELDS, rows, 256), jnp.bfloat16),
            pltpu.VMEM((FIELDS, rows, 256), jnp.bfloat16),
            pltpu.VMEM((FIELDS, rows, 256), jnp.float32),
            pltpu.VMEM((FIELDS, rows, 384), jnp.float32),
            pltpu.VMEM((OLD_CAP,) + box, jnp.float32),
            pltpu.VMEM((BOX_DEV,) + box, jnp.float32),
            pltpu.VMEM((2, FIELDS, 2, CX, 128), jnp.float32),
            pltpu.VMEM((2, CX, 128), jnp.float32),
            pltpu.VMEM((2, 2, CX + 16, CY), jnp.float32),
            pltpu.VMEM((5, CX, CY), jnp.float32),
            pltpu.VMEM((2, CX, 128), jnp.float32),
            pltpu.SMEM(((CX // HALF) * (CY // HALF),), jnp.int32),
            pltpu.SMEM((peers * MOVE_CAP,), jnp.int32),
            pltpu.SMEM((peers,), jnp.int32),
            pltpu.SMEM((OLD_CAP,), jnp.int32),
            pltpu.SemaphoreType.DMA((5,)),
            pltpu.SemaphoreType.DMA((3,)),
            pltpu.SemaphoreType.DMA((6,)),
            pltpu.SemaphoreType.DMA((4,)),
            pltpu.SemaphoreType.DMA,
        ],
        compiler_params=whole,
        cost_estimate=pl.CostEstimate(flops=10**9, bytes_accessed=60 * 10**6, transcendentals=0),
    )(
        *integers, later, jnp.asarray(GROW), jnp.asarray(MEAN), jnp.asarray(FACE), fine,
        *stash, cols_plus, cols_minus,
    )
    fine_new, coarse_new = pl.pallas_call(
        finish_kernel,
        out_shape=(
            jax.ShapeDtypeStruct((BOX_DEV,) + box, jnp.float32),
            jax.ShapeDtypeStruct(coarse.shape, coarse.dtype),
        ),
        in_specs=[hbm, vmem, vmem, hbm, hbm],
        out_specs=(hbm, hbm),
        scratch_shapes=[
            pltpu.VMEM((peers, MOVE_CAP * ROWS, 128), jnp.float32),
            pltpu.VMEM((FIELDS, 2, 8, CY), jnp.float32),
            pltpu.SMEM((peers, 8, 128), jnp.float32),
            pltpu.SemaphoreType.DMA,
            pltpu.SemaphoreType.DMA((peers,)),
            pltpu.SemaphoreType.DMA((peers, MOVE_CAP)),
            pltpu.SemaphoreType.DMA((2, FIELDS)),
        ],
        input_output_aliases={3: 0, 4: 1},
        compiler_params=small,
        cost_estimate=pl.CostEstimate(flops=0, bytes_accessed=5 * 10**6, transcendentals=0),
    )(arrived, rows_plus, rows_minus, fine_part, coarse_part)
    fine_new = fine_new.reshape(BOX_DEV, FIELDS, 8, BZ, 128).transpose(0, 1, 3, 2, 4)
    return coarse_new, fine_new.reshape(BOX_DEV, FIELDS, BZ, BX * BX)


def solution(mesh):
    return jax.shard_map(
        per_device,
        mesh=mesh,
        in_specs=(
            P(None, None, "gx", "gy"),
            P(("gx", "gy"), None, None, None),
            P(("gx", "gy")),
            P(None, ("gx", "gy")),
            P(("gx", "gy")),
            P(("gx", "gy")),
            P(("gx", "gy")),
        ),
        out_specs=(P(None, None, "gx", "gy"), P(("gx", "gy"), None, None, None)),
        check_vma=False,
    )
```
